256 devices in a mesh: tile: 32 (over x_lo, z, core), win: 8 (over y, x_hi).
Axes of the slice: x: 4 (x_hi: 2, x_lo: 2; x = x_hi * 2 + x_lo), y: 4, z: 8, core: 2. Of those that a mesh axis runs over, the one named last changes fastest.
Arguments:
- spectra: float32 [4, 128, 2, 4096], P(None, 'win', None, 'tile'), may hold values from -6 to 6
- sensor_positions: float32 [2, 4096], replicated, may hold values from -600 to 600
- wavenumbers: float32 [4], replicated, may hold values from 0.02 to 0.2
- sensor_order: int32 [4096], replicated, may hold values from 0 to 4095, each once
- candidates: int32 [4, 1024], replicated, may hold values from 0 to 4095
Outputs:
- csd: float32 [4, 2, 4096, 4096], P(None, None, 'tile', 'win')
- beam: float32 [4, 1024], P(None, ('tile', 'win'))
The draws below stay inside these ranges and needn't reach their ends.
Inputs may be any that keep to these rules, and one draw needn't show every extreme that they name: `sensor_order`: each acquisition index appears exactly once.
All inputs are finite; a program needn't handle non-finite values.
Results may differ from the reference program's by a relative error of at most 0.0002.
Values sent between devices are 32-bit elements; how exact they have to be, the bound alone decides.
No kernel may reach another device: no remote copies, remote signals or barrier semaphores. Data moves between devices by JAX's collectives and lax.ppermute only.
A program may use at most 128 MiB of HBM per device.

```python
import math
import jax
import jax.numpy as jnp
from jax import lax

S = 4096
F = 4
C = 1024
GRID_SIDE = 64
W = 128


def set_ends(entries, key, least, high):
    dims = entries.shape
    place = [jax.random.randint(jax.random.fold_in(key, axis), (), 0, dims[axis]) for axis in range(len(dims))]
    entries = entries.at[tuple(place)].set(least)
    longest = dims.index(max(dims))
    place[longest] = (place[longest] + 1) % dims[longest]
    return entries.at[tuple(place)].set(high)


def shard_levels(own_key, extent, shards, smallest, largest):
    def one(dim, shards_of):
        steps = jax.random.uniform(jax.random.fold_in(jax.random.fold_in(own_key, 6), dim), (shards_of,), jnp.float32, smallest / len(shards), largest / len(shards))
        return jnp.repeat(jnp.exp(steps), extent[dim] // shards_of).reshape((-1,) + (1,) * (len(extent) - dim - 1))

    loudness = one(*shards[0])
    for cut in shards[1:]:
        loudness = loudness * one(*cut)
    return loudness


def noise(rng, extent, width, reach, pieces=(), dtype=jnp.bfloat16):
    result = width * jax.random.normal(rng, extent, jnp.float32)
    if pieces:
        result = result * shard_levels(rng, extent, pieces, -0.22, 0.18)
    return jnp.clip(result, -reach, reach).astype(dtype)


def setup_inputs(seed: int = 0) -> dict:
    key_list = jax.random.split(jax.random.key(seed), 6)
    spectra = noise(key_list[0], (F, W, 2, S), 1.0, 6.0, ((1, 8), (3, 32)), jnp.float32)
    sensor_positions = jnp.clip(jax.random.uniform(key_list[1], (2, S), jnp.float32, -600.0, 600.0), -600.0, 600.0)
    wavenumbers = jnp.clip(jnp.exp(jax.random.uniform(key_list[2], (F,), jnp.float32, math.log(0.02), math.log(0.2))), 0.02, 0.2)
    sensor_order = jax.random.permutation(key_list[3], S).astype(jnp.int32)
    candidates = set_ends(jax.random.randint(key_list[4], (F, C), 0, GRID_SIDE * GRID_SIDE), jax.random.fold_in(key_list[4], 1), 0, (GRID_SIDE * GRID_SIDE) - 1).astype(jnp.int32)
    return {"spectra": spectra, "sensor_positions": sensor_positions, "wavenumbers": wavenumbers, "sensor_order": sensor_order, "candidates": candidates}


def replica(pos_x, pos_y, cand, wave):
    cand_x = ((cand % GRID_SIDE).astype(jnp.float32) - GRID_SIDE / 2) * 8.0
    cand_z = 50.0 + (cand // GRID_SIDE).astype(jnp.float32) * 4.0
    delta = pos_x[:, None] - cand_x[None, :]
    radius = jnp.sqrt(delta * delta + (pos_y * pos_y)[:, None] + (cand_z * cand_z)[None, :])
    amplitude = 1.0 / radius
    phase = wave * radius
    return (amplitude * jnp.cos(phase), -amplitude * jnp.sin(phase), amplitude)

def reference(spectra, sensor_positions, wavenumbers, sensor_order, candidates):
    total = spectra.shape[1]
    ordered = jnp.take(spectra, sensor_order, axis=3)
    pos_x = jnp.take(sensor_positions[0], sensor_order)
    pos_y = jnp.take(sensor_positions[1], sensor_order)
    hp = lax.Precision.HIGHEST
    dens_list = []
    beam_list = []
    for freq in range(F):
        real_part = ordered[freq, :, 0]
        imag_part = ordered[freq, :, 1]
        dens_re = (jnp.dot(real_part.T, real_part, precision=hp) + jnp.dot(imag_part.T, imag_part, precision=hp)) / total
        dens_im = (jnp.dot(imag_part.T, real_part, precision=hp) - jnp.dot(real_part.T, imag_part, precision=hp)) / total
        dens_list.append(jnp.stack([dens_re, dens_im]))
        rep_re, rep_im, amplitude = replica(pos_x, pos_y, candidates[freq], wavenumbers[freq])
        proj_re = jnp.dot(real_part, rep_re, precision=hp) + jnp.dot(imag_part, rep_im, precision=hp)
        proj_im = jnp.dot(imag_part, rep_re, precision=hp) - jnp.dot(real_part, rep_im, precision=hp)
        power = lax.optimization_barrier(jnp.sum(proj_re * proj_re + proj_im * proj_im, axis=0)) / total
        norm = lax.optimization_barrier(jnp.sum(amplitude * amplitude, axis=0))
        beam_list.append(power / norm)
    return (jnp.stack(dens_list), jnp.stack(beam_list))
```

```python
import jax
import jax.numpy as jnp
import numpy as np
from jax import lax
from jax.experimental import pallas as pl
from jax.experimental.pallas import tpu as pltpu
from jax.sharding import Mesh, PartitionSpec as P

GRID_SIDE = 64
SENSORS = 4096
WINDOWS = 128
LANES = 128
SEGS = SENSORS // LANES
ROWS = 32
DESTS = 32
CANDS = 128
MSG = 3 * ROWS + 8
TILE = ("xl", "z", "core")
PLANE = ("xl", "core", "y", "xh")


def turn_series():
    x = np.cos(np.linspace(0.0, np.pi, 4001)) * 0.5
    y = x * x
    powers = y[:, None] ** np.arange(8)[None, :]
    cos_c = np.linalg.lstsq(powers, np.cos(2 * np.pi * x), rcond=None)[0]
    sinc = 2 * np.pi * np.sinc(2 * x)
    sin_c = np.linalg.lstsq(powers, sinc, rcond=None)[0]
    return [float(v) for v in cos_c], [float(v) for v in sin_c]


COS_C, SIN_C = turn_series()


def split(value):
    high = value.astype(jnp.bfloat16)
    low = (value - high.astype(jnp.float32)).astype(jnp.bfloat16)
    return high, low


def swap_pairs(value):
    count = value.shape[0]
    up = pltpu.roll(value, count - 1, 0)
    down = pltpu.roll(value, 1, 0)
    row = lax.broadcasted_iota(jnp.int32, value.shape, 0)
    return jnp.where(row % 2 == 0, up, -down)


def replica_kernel(turn_ref, pos_ref, cx_ref, cz_ref, high_ref, low_ref, scale_ref, acc):
    turn = turn_ref[0]
    acc[...] = jnp.zeros_like(acc)

    @pl.loop(0, SEGS // 2)
    def _(pair):
        for half in range(2):
            seg = pair * 2 + half
            px = pos_ref[0, pl.ds(seg, 1), :]
            py = pos_ref[1, pl.ds(seg, 1), :]
            py2 = py * py
            for part in range(CANDS // 32):
                own = slice(part * 32, part * 32 + 32)
                delta = px - cx_ref[own, :]
                cz = cz_ref[own, :]
                r2 = delta * delta + py2 + cz * cz
                inv = lax.rsqrt(r2)
                turns = (r2 * inv) * turn
                x = turns - jnp.round(turns)
                y = x * x
                cos = jnp.full_like(y, COS_C[7])
                sin = jnp.full_like(y, SIN_C[7])
                for power in range(6, -1, -1):
                    cos = cos * y + COS_C[power]
                    sin = sin * y + SIN_C[power]
                re_h, re_l = split(inv * cos)
                im_h, im_l = split(-(inv * x) * sin)
                lanes = slice(half * LANES, half * LANES + LANES)
                own_im = slice(CANDS + part * 32, CANDS + part * 32 + 32)
                high_ref[pair, own, lanes] = re_h
                low_ref[pair, own, lanes] = re_l
                high_ref[pair, own_im, lanes] = im_h
                low_ref[pair, own_im, lanes] = im_l
                acc[own, :] += inv * inv

    norm = jnp.sum(acc[...].T, axis=0, keepdims=True)
    scale_ref[...] = jnp.broadcast_to(1.0 / (WINDOWS * norm), (8, CANDS))


def make_replicas(turn, positions, cand_x, cand_z):
    full = lambda *s: pl.BlockSpec(memory_space=pltpu.VMEM)
    return pl.pallas_call(
        replica_kernel,
        out_shape=(
            jax.ShapeDtypeStruct((SEGS // 2, 2 * CANDS, 2 * LANES), jnp.bfloat16),
            jax.ShapeDtypeStruct((SEGS // 2, 2 * CANDS, 2 * LANES), jnp.bfloat16),
            jax.ShapeDtypeStruct((8, CANDS), jnp.float32),
        ),
        in_specs=[pl.BlockSpec(memory_space=pltpu.SMEM)] + [full()] * 3,
        out_specs=(full(), full(), full()),
        scratch_shapes=[pltpu.VMEM((CANDS, LANES), jnp.float32)],
        compiler_params=pltpu.CompilerParams(vmem_limit_bytes=32 * 1024 * 1024),
        cost_estimate=pl.CostEstimate(flops=30_000_000, bytes_accessed=5_000_000, transcendentals=600_000),
        name="replicas",
    )(turn, positions, cand_x, cand_z)


def pack_kernel(z_ref, order_ref, spec_ref, high_ref, low_ref, scale_ref, out_ref, held, proj):
    contract = (((1,), (1,)), ((), ()))
    proj[...] = jnp.zeros_like(proj)

    @pl.loop(0, SEGS // 2)
    def _(pair):
        data = jnp.concatenate([spec_ref[pair * 2], spec_ref[pair * 2 + 1]], axis=1)
        data_h, data_l = split(data)
        both = jnp.concatenate([data_h, data_l], axis=0)
        first = lax.dot_general(both, high_ref[pair], contract, preferred_element_type=jnp.float32)
        second = lax.dot_general(data_h, low_ref[pair], contract, preferred_element_type=jnp.float32)
        proj[...] += first[:ROWS] + first[ROWS:] + second
        for half in range(2):
            seg = pair * 2 + half
            index = jnp.broadcast_to(order_ref[pl.ds(seg, 1), :], (ROWS, LANES))
            lane = index % LANES
            home = index // LANES
            total = jnp.zeros((ROWS, LANES), jnp.float32)
            for run in range(SEGS):
                there = jnp.take_along_axis(spec_ref[run], lane, axis=1)
                total = jnp.where(home == run, there, total)
            held[seg] = total

    value = proj[:, :CANDS] + swap_pairs(proj[:, CANDS:])
    power = jnp.sum(value * value, axis=0, keepdims=True) * scale_ref[...]
    z = z_ref[0]
    for xl in range(2):
        for core in range(2):
            mine = held[xl * 16 + z * 2 + core]
            for block in range(8):
                dest = (xl * 2 + core) * 8 + block
                out_ref[dest, 0:ROWS, :] = mine
                for run in range(2):
                    out_ref[dest, (1 + run) * ROWS:(2 + run) * ROWS, :] = held[block * 4 + core * 2 + run]
                out_ref[dest, 3 * ROWS:, :] = power


def make_messages(z, order, spec, high, low, scale):
    full = lambda: pl.BlockSpec(memory_space=pltpu.VMEM)
    return pl.pallas_call(
        pack_kernel,
        out_shape=jax.ShapeDtypeStruct((DESTS, MSG, LANES), jnp.float32),
        in_specs=[pl.BlockSpec(memory_space=pltpu.SMEM)] + [full()] * 5,
        out_specs=full(),
        scratch_shapes=[
            pltpu.VMEM((SEGS, ROWS, LANES), jnp.float32),
            pltpu.VMEM((ROWS, 2 * CANDS), jnp.float32),
        ],
        compiler_params=pltpu.CompilerParams(vmem_limit_bytes=32 * 1024 * 1024),
        cost_estimate=pl.CostEstimate(flops=200_000_000, bytes_accessed=6_000_000, transcendentals=0),
        name="messages",
    )(z, order, spec, high, low, scale)


def density_kernel(core_ref, own_ref, other_ref, out_ref):
    depth = 8 * ROWS
    rows = own_ref[0, :, 0:ROWS, :].reshape(depth, LANES) * (1.0 / WINDOWS)
    left = jnp.concatenate([rows, swap_pairs(rows)], axis=1)
    left_h, left_l = split(left.T)
    contract = (((1,), (0,)), ((), ()))
    core = core_ref[0]
    for half, source, base in ((core, own_ref, ROWS), (1 - core, other_ref, 0)):
        parts = [source[0, :, base + run * ROWS:base + (run + 1) * ROWS, :].reshape(depth, LANES) for run in range(2)]
        right_h, right_l = split(jnp.concatenate(parts, axis=1))
        total = lax.dot_general(left_h, right_h, contract, preferred_element_type=jnp.float32)
        total += lax.dot_general(left_h, right_l, contract, preferred_element_type=jnp.float32)
        total += lax.dot_general(left_l, right_h, contract, preferred_element_type=jnp.float32)
        place = pl.ds(pl.multiple_of(half * 2 * LANES, 2 * LANES), 2 * LANES)
        out_ref[0, 0, :, place] = total[:LANES]
        out_ref[0, 1, :, place] = total[LANES:]


def make_density(core, own, other):
    freqs = own.shape[0]
    return pl.pallas_call(
        density_kernel,
        grid=(freqs,),
        out_shape=jax.ShapeDtypeStruct((freqs, 2, LANES, 4 * LANES), jnp.float32),
        in_specs=[
            pl.BlockSpec(memory_space=pltpu.SMEM),
            pl.BlockSpec((1, 8, MSG, LANES), lambda f: (f, 0, 0, 0)),
            pl.BlockSpec((1, 8, 2 * ROWS, LANES), lambda f: (f, 0, 0, 0)),
        ],
        out_specs=pl.BlockSpec((1, 2, LANES, 4 * LANES), lambda f: (f, 0, 0, 0)),
        compiler_params=pltpu.CompilerParams(vmem_limit_bytes=32 * 1024 * 1024),
        name="density",
    )(core, own, other)


def local(spectra, sensor_positions, wavenumbers, sensor_order, candidates):
    xl, z, core = (lax.axis_index(name) for name in TILE)
    freq = xl * 2 + core
    outgoing = jnp.broadcast_to(spectra.reshape(2, 1, 2, ROWS, LANES), (2, 8, 2, ROWS, LANES))
    gathered = lax.all_to_all(outgoing.reshape(DESTS, ROWS, LANES), TILE, 0, 0, tiled=True)
    grid = lax.dynamic_index_in_dim(candidates, freq, 0, keepdims=False)
    grid = lax.dynamic_index_in_dim(grid.reshape(2, 8, 2, 32), z, 1, keepdims=False).reshape(CANDS, 1)
    cand_x = ((grid % GRID_SIDE).astype(jnp.float32) - GRID_SIDE / 2) * 8.0
    cand_z = 50.0 + (grid // GRID_SIDE).astype(jnp.float32) * 4.0
    turn = lax.dynamic_slice_in_dim(wavenumbers, freq, 1) * (0.5 / np.pi)
    high, low, scale = make_replicas(
        turn.astype(jnp.float32),
        sensor_positions.reshape(2, SEGS, LANES),
        jnp.broadcast_to(cand_x, (CANDS, LANES)),
        jnp.broadcast_to(cand_z, (CANDS, LANES)),
    )
    messages = make_messages(z.reshape(1), sensor_order.reshape(SEGS, LANES), gathered, high, low, scale)
    received = lax.all_to_all(messages, PLANE, 0, 0, tiled=True).reshape(4, 8, MSG, LANES)
    columns = received[:, :, ROWS:3 * ROWS, :]
    other = lax.ppermute(columns, "core", [(0, 1), (1, 0)])
    density = make_density(core.reshape(1), received, other)
    shares = jnp.sum(received[:, :, 3 * ROWS, :], axis=1)
    mine = lax.axis_index(PLANE) * 4
    beam = lax.dynamic_slice_in_dim(shares, mine, 4, 1)
    return (density, beam)


def solution(mesh):
    fine = Mesh(mesh.devices.reshape(2, 8, 2, 4, 2), ("xl", "z", "core", "y", "xh"))
    in_specs = (P(None, ("y", "xh"), None, TILE), P(), P(), P(), P())
    out_specs = (P(None, None, TILE, ("y", "xh")), P(None, TILE + ("y", "xh")))
    return jax.shard_map(local, mesh=fine, in_specs=in_specs, out_specs=out_specs, check_vma=False)
```

```python
import jax
import jax.numpy as jnp
import numpy as np
from jax import lax
from jax.experimental import pallas as pl
from jax.experimental.pallas import tpu as pltpu
from jax.sharding import Mesh, PartitionSpec as P

GRID_SIDE = 64
WINDOWS = 128
LANES = 128
SEGS = 32
ROWS = 16
PEERS = 64
MSG = 3 * ROWS + 2
VMEM_LIMIT = 24 * 1024 * 1024
NAMES = ("xl", "zh", "zl", "core", "y", "xh")
SIZES = (2, 4, 2, 2, 4, 2)
TILE = ("xl", "zh", "zl", "core")
WIN = ("y", "xh")
GATHER = ("core", "xl", "zh", "zl")
SPREAD = ("y", "xl", "xh", "zl", "core")

PEER = [(y, xl, xh, zl, core) for y in range(4) for xl in range(2) for xh in range(2) for zl in range(2) for core in range(2)]
HOLDERS = [[n for n, p in enumerate(PEER) if p[4] * 2 + p[1] == freq] for freq in range(4)]


def tile_of(run):
    return (run % 16) * 2 + run // 16


def half_turn_series():
    x = np.cos(np.linspace(0.0, np.pi, 4001)) * 0.5
    y = x * x
    powers = y[:, None] ** np.arange(5)[None, :]
    sin_c = np.linalg.lstsq(powers[:, :5], np.sqrt(2.0) * np.pi * np.sinc(x), rcond=None)[0]
    cos_c = np.linalg.lstsq(powers[:, :5], -np.sqrt(2.0) * np.cos(np.pi * x), rcond=None)[0]
    return [float(v) for v in sin_c], [float(v) for v in cos_c]


SIN_C, COS_C = half_turn_series()


def series(coefficients, y):
    total = coefficients[-1] * y + coefficients[-2]
    for c in coefficients[-3::-1]:
        total = total * y + c
    return total


def in_vmem():
    return pl.BlockSpec(memory_space=pltpu.VMEM)


def in_hbm():
    return pl.BlockSpec(memory_space=pltpu.HBM)


def keep_in_hbm(array):
    return pltpu.with_memory_space_constraint(array, pltpu.HBM)


def my_freq():
    return lax.axis_index("core") * 2 + lax.axis_index("xl")


def split(value):
    high = value.astype(jnp.bfloat16)
    low = (value - high.astype(jnp.float32)).astype(jnp.bfloat16)
    return high, low


def swap_pairs(value):
    count = value.shape[0]
    up = pltpu.roll(value, count - 1, 0)
    down = pltpu.roll(value, 1, 0)
    row = lax.broadcasted_iota(jnp.int32, value.shape, 0)
    return jnp.where(row % 2 == 0, up, -down)


def replica_kernel(pos_hbm, cand_hbm, wave_hbm, high_hbm, low_hbm, pos_ref, cand_ref, wave_ref, high_ref, low_ref, sem):
    pairs = ((pos_hbm, pos_ref), (cand_hbm, cand_ref), (wave_hbm, wave_ref))
    loads = [pltpu.make_async_copy(src, dst, sem.at[2 + n]) for n, (src, dst) in enumerate(pairs)]
    for load in loads:
        load.start()
    for load in loads:
        load.wait()
    freq, zh = my_freq(), lax.axis_index("zh")
    turn = wave_ref[freq] * (0.5 / np.pi)
    cx, cz2 = [], []
    for xl in range(2):
        lanes = pl.ds(pl.multiple_of((xl * 4 + zh) * LANES, LANES), LANES)
        grids = cand_ref[:, lanes]
        bin_of = lax.broadcasted_iota(jnp.int32, grids.shape, 0)
        grid = jnp.sum(jnp.where(bin_of == freq, grids, 0), axis=0, keepdims=True)
        cx.append(((grid % GRID_SIDE).astype(jnp.float32) - GRID_SIDE / 2) * 8.0)
        depth = 50.0 + (grid // GRID_SIDE).astype(jnp.float32) * 4.0
        cz2.append(depth * depth)

    def stores(pair):
        return [
            pltpu.make_async_copy(src.at[pair], dst.at[pair], sem.at[n])
            for n, (src, dst) in enumerate(((high_ref, high_hbm), (low_ref, low_hbm)))
        ]

    @pl.loop(0, SEGS // 2)
    def _(pair):
        for half in range(2):
            lanes = pl.ds(pl.multiple_of(tile_of(pair * 2 + half) * LANES, LANES), LANES)
            px = jnp.broadcast_to(pos_ref[0:1, lanes], (LANES, LANES)).T
            py = pos_ref[1:2, lanes]
            py2 = jnp.broadcast_to(py * py, (LANES, LANES)).T
            for xl in range(2):
                for part in range(LANES // 32):
                    own = slice(part * 32, part * 32 + 32)
                    delta = px[own] - cx[xl]
                    r2 = delta * delta + (py2[own] + cz2[xl])
                    inv = lax.rsqrt(r2)
                    turns = (r2 * inv) * turn
                    x = turns - jnp.round(turns)
                    y = x * x
                    sin = x * series(SIN_C, y)
                    most = inv * sin
                    re_h, re_l = split(inv - most * sin)
                    im_h, im_l = split(most * series(COS_C, y))
                    rows = slice(half * LANES + part * 32, half * LANES + part * 32 + 32)
                    re = slice(xl * 2 * LANES, xl * 2 * LANES + LANES)
                    im = slice(xl * 2 * LANES + LANES, xl * 2 * LANES + 2 * LANES)
                    high_ref[pair, rows, re] = re_h
                    low_ref[pair, rows, re] = re_l
                    high_ref[pair, rows, im] = im_h
                    low_ref[pair, rows, im] = im_l
        for store in stores(pair):
            store.start()

    @pl.loop(0, SEGS // 2)
    def _(pair):
        for store in stores(pair):
            store.wait()


def make_replicas(positions, cands, wavenumbers):
    replicas = pltpu.HBM((SEGS // 2, 2 * LANES, 4 * LANES), jnp.bfloat16)
    return pl.pallas_call(
        replica_kernel,
        out_shape=(replicas, replicas),
        in_specs=[in_hbm()] * 3,
        out_specs=(in_hbm(), in_hbm()),
        scratch_shapes=[
            pltpu.VMEM(positions.shape, jnp.float32),
            pltpu.VMEM(cands.shape, jnp.int32),
            pltpu.SMEM(wavenumbers.shape, jnp.float32),
            pltpu.VMEM(replicas.shape, jnp.bfloat16),
            pltpu.VMEM(replicas.shape, jnp.bfloat16),
            pltpu.SemaphoreType.DMA((5,)),
        ],
        compiler_params=pltpu.CompilerParams(vmem_limit_bytes=VMEM_LIMIT),
        cost_estimate=pl.CostEstimate(flops=60_000_000, bytes_accessed=10_000_000, transcendentals=1_000_000),
        name="replicas",
    )(*[keep_in_hbm(array) for array in (positions, cands, wavenumbers)])


def message_kernel(order_ref, spec_ref, high_hbm, low_hbm, out_ref, held, high_ref, low_ref, sem):
    zh = lax.axis_index("zh")

    def loads(some):
        two = pl.ds(some * 2, 2)
        return [
            pltpu.make_async_copy(src.at[two], dst.at[two], sem.at[n, some])
            for n, (src, dst) in enumerate(((high_hbm, high_ref), (low_hbm, low_ref)))
        ]

    for some in range(SEGS // 4):
        for load in loads(some):
            load.start()
    proj = jnp.zeros((ROWS, 4 * LANES), jnp.float32)
    for some in range(SEGS // 4):
        for seg in range(some * 4, some * 4 + 4):
            index = jnp.broadcast_to(order_ref[seg:seg + 1, :], (8, LANES))
            lane = index % LANES
            home = index // LANES
            total = [jnp.zeros((8, LANES), jnp.float32) for _ in range(ROWS // 8)]
            for run in range(SEGS):
                here = home == tile_of(run)
                for part in range(ROWS // 8):
                    there = jnp.take_along_axis(spec_ref[run, part * 8:part * 8 + 8, :], lane, axis=1)
                    total[part] = jnp.where(here, there, total[part])
            for part in range(ROWS // 8):
                held[seg, part * 8:part * 8 + 8, :] = total[part]
        for load in loads(some):
            load.wait()
        for pair in range(some * 2, some * 2 + 2):
            data = jnp.concatenate([spec_ref[pair * 2], spec_ref[pair * 2 + 1]], axis=1)
            data_h, data_l = split(data)
            both = jnp.concatenate([data_h, data_l], axis=0)
            first = jnp.dot(both, high_ref[pair], preferred_element_type=jnp.float32)
            second = jnp.dot(data_h, low_ref[pair], preferred_element_type=jnp.float32)
            proj += first[:ROWS] + first[ROWS:] + second

    powers = []
    for xl in range(2):
        real = proj[:, xl * 2 * LANES:xl * 2 * LANES + LANES]
        value = real + swap_pairs(proj[:, xl * 2 * LANES + LANES:xl * 2 * LANES + 2 * LANES])
        powers.append(jnp.sum(value * value, axis=0, keepdims=True))
    for peer, (y, xl, xh, zl, core) in enumerate(PEER):
        start = peer * MSG
        out_ref[start:start + ROWS, :] = held[xl * 16 + zh * 4 + zl * 2 + core]
        for run in range(2):
            place = slice(start + (1 + run) * ROWS, start + (2 + run) * ROWS)
            out_ref[place, :] = held[(y * 2 + xh) * 4 + core * 2 + run]
        out_ref[start + 3 * ROWS:start + MSG, :] = jnp.broadcast_to(powers[xl], (MSG - 3 * ROWS, LANES))


def make_messages(order, spec, high, low):
    return pl.pallas_call(
        message_kernel,
        out_shape=jax.ShapeDtypeStruct((PEERS * MSG, LANES), jnp.float32),
        in_specs=[in_vmem(), in_vmem(), in_hbm(), in_hbm()],
        out_specs=in_vmem(),
        scratch_shapes=[
            pltpu.VMEM((SEGS, ROWS, LANES), jnp.float32),
            pltpu.VMEM(high.shape, high.dtype),
            pltpu.VMEM(low.shape, low.dtype),
            pltpu.SemaphoreType.DMA((2, SEGS // 4)),
        ],
        compiler_params=pltpu.CompilerParams(vmem_limit_bytes=VMEM_LIMIT),
        cost_estimate=pl.CostEstimate(flops=100_000_000, bytes_accessed=10_000_000, transcendentals=0),
        name="messages",
    )(order, spec, keep_in_hbm(high), keep_in_hbm(low))


def gather_rows(ref, freq, start):
    each = ref.shape[0] // PEERS
    return jnp.concatenate([ref[n * each + start:n * each + start + ROWS, :] for n in HOLDERS[freq]], axis=0)


def product(left_h, left_l, ref, freq, start):
    parts = [gather_rows(ref, freq, start + run * ROWS) for run in range(2)]
    right_h, right_l = split(jnp.concatenate(parts, axis=1))
    total = jnp.dot(left_h, right_h, preferred_element_type=jnp.float32)
    total += jnp.dot(left_h, right_l, preferred_element_type=jnp.float32)
    return total + jnp.dot(left_l, right_h, preferred_element_type=jnp.float32)


def send_out(freq, half, total, stage, out_ref, sem):
    stage[freq, 0] = total[:LANES]
    stage[freq, 1] = total[LANES:]
    columns = pl.ds(pl.multiple_of(half * 2 * LANES, 2 * LANES), 2 * LANES)
    copy = pltpu.make_async_copy(stage.at[freq], out_ref.at[freq, :, :, columns], sem.at[freq])
    copy.start()
    return copy


def own_density_kernel(got_ref, out_ref, high_ref, low_ref, stage, sem):
    copies = []
    for freq in range(4):
        rows = gather_rows(got_ref, freq, 0) * (1.0 / WINDOWS)
        left = jnp.concatenate([rows, swap_pairs(rows)], axis=1)
        left_h, left_l = split(left.T)
        high_ref[freq] = left_h
        low_ref[freq] = left_l
        total = product(left_h, left_l, got_ref, freq, ROWS)
        copies.append(send_out(freq, lax.axis_index("core"), total, stage, out_ref, sem))
    for copy in copies:
        copy.wait()


def other_density_kernel(high_ref, low_ref, got_ref, base_ref, out_ref, stage, sem):
    del base_ref
    copies = []
    for freq in range(4):
        total = product(high_ref[freq], low_ref[freq], got_ref, freq, 0)
        copies.append(send_out(freq, 1 - lax.axis_index("core"), total, stage, out_ref, sem))
    for copy in copies:
        copy.wait()


def make_density(received, columns):
    density = jax.ShapeDtypeStruct((4, 2, LANES, 4 * LANES), jnp.float32)
    left = jax.ShapeDtypeStruct((4, 2 * LANES, 2 * LANES), jnp.bfloat16)
    scratch = [pltpu.VMEM((4, 2, LANES, 2 * LANES), jnp.float32), pltpu.SemaphoreType.DMA((4,))]
    params = pltpu.CompilerParams(vmem_limit_bytes=VMEM_LIMIT)
    cost = pl.CostEstimate(flops=800_000_000, bytes_accessed=5_000_000, transcendentals=0)
    anywhere = in_hbm()
    half, high, low = pl.pallas_call(
        own_density_kernel,
        out_shape=(density, left, left),
        in_specs=[in_vmem()],
        out_specs=(anywhere, in_vmem(), in_vmem()),
        scratch_shapes=scratch,
        compiler_params=params,
        cost_estimate=cost,
        name="own_density",
    )(received)
    other = lax.ppermute(columns, "core", [(0, 1), (1, 0)])
    return pl.pallas_call(
        other_density_kernel,
        out_shape=density,
        in_specs=[in_vmem(), in_vmem(), in_vmem(), anywhere],
        out_specs=anywhere,
        scratch_shapes=scratch,
        input_output_aliases={3: 0},
        compiler_params=params,
        cost_estimate=cost,
        name="other_density",
    )(high, low, other, half)


def norms_of(positions, cands):
    cand_x = ((cands % GRID_SIDE).astype(jnp.float32) - GRID_SIDE / 2) * 8.0
    cand_z = 50.0 + (cands // GRID_SIDE).astype(jnp.float32) * 4.0
    delta = positions[0] - cand_x[..., None]
    r2 = delta * delta + positions[1] * positions[1] + (cand_z * cand_z)[..., None]
    return jnp.sum(1.0 / r2, axis=-1)


def local(spectra, sensor_positions, wavenumbers, sensor_order, candidates):
    parts = spectra.reshape(2, 2, 1, 2, ROWS, LANES)
    outgoing = jnp.broadcast_to(parts, (2, 2, 4, 2, ROWS, LANES))
    gathered = lax.all_to_all(outgoing.reshape(SEGS, ROWS, LANES), GATHER, 0, 0, tiled=True)
    high, low = make_replicas(sensor_positions, candidates, wavenumbers)
    messages = make_messages(sensor_order.reshape(SEGS, LANES), gathered, high, low)
    received = lax.all_to_all(messages.reshape(PEERS, MSG // 2, 2, LANES), SPREAD, 0, 0, tiled=True)
    columns = received[:, ROWS // 2:3 * ROWS // 2].reshape(PEERS * 2 * ROWS, LANES)
    density = make_density(received.reshape(PEERS * MSG, LANES), columns)
    shares = received[:, 3 * ROWS // 2, 0, :].reshape(4, 2, 2, 2, 2, LANES)
    powers = jnp.sum(shares, axis=(0, 2, 3)).swapaxes(0, 1).reshape(4, LANES)
    win = lax.axis_index(WIN)
    power = lax.dynamic_slice_in_dim(powers, (lax.axis_index(("zl", "core")) * 8 + win) * 4, 4, 1)
    candidates, _ = lax.optimization_barrier((candidates, power))
    owned = lax.dynamic_slice_in_dim(candidates, (lax.axis_index(TILE) * 8 + win) * 4, 4, 1)
    beam = power / (WINDOWS * norms_of(sensor_positions, owned))
    return (density, beam)


def solution(mesh):
    fine = Mesh(mesh.devices.reshape(SIZES), NAMES)
    in_specs = (P(None, WIN, None, TILE), P(), P(), P(), P())
    out_specs = (P(None, None, TILE, WIN), P(None, TILE + WIN))
    return jax.shard_map(local, mesh=fine, in_specs=in_specs, out_specs=out_specs, check_vma=False)
```

```python
import jax
import jax.numpy as jnp
import numpy as np
from jax import lax
from jax.experimental import pallas as pl
from jax.experimental.pallas import tpu as pltpu
from jax.sharding import Mesh, PartitionSpec as P

GRID_SIDE = 64
WINDOWS = 128
LANES = 128
SEGS = 32
ROWS = 16
PEERS = 64
MSG = 3 * ROWS + 2
VMEM_LIMIT = 24 * 1024 * 1024
UNROLL = 4
PAIRS = SEGS // 2
HELD = 6
NAMES = ("xl", "zh", "zl", "core", "y", "xh")
SIZES = (2, 4, 2, 2, 4, 2)
TILE = ("xl", "zh", "zl", "core")
WIN = ("y", "xh")
GATHER = ("core", "xl", "zh", "zl")
SPREAD = ("y", "xl", "xh", "zl", "core")

PEER = [(y, xl, xh, zl, core) for y in range(4) for xl in range(2) for xh in range(2) for zl in range(2) for core in range(2)]
HOLDERS = [[n for n, p in enumerate(PEER) if p[4] * 2 + p[1] == freq] for freq in range(4)]


def tile_of(run):
    return (run % 16) * 2 + run // 16


def half_turn_series():
    x = np.cos(np.linspace(0.0, np.pi, 4001)) * 0.5
    y = x * x
    powers = y[:, None] ** np.arange(5)[None, :]
    sin_c = np.linalg.lstsq(powers[:, :5], np.sqrt(2.0) * np.pi * np.sinc(x), rcond=None)[0]
    cos_c = np.linalg.lstsq(powers[:, :5], -np.sqrt(2.0) * np.cos(np.pi * x), rcond=None)[0]
    return [float(v) for v in sin_c], [float(v) for v in cos_c]


SIN_C, COS_C = half_turn_series()


def series(coefficients, y):
    total = coefficients[-1] * y + coefficients[-2]
    for c in coefficients[-3::-1]:
        total = total * y + c
    return total


def in_vmem():
    return pl.BlockSpec(memory_space=pltpu.VMEM)


def in_hbm():
    return pl.BlockSpec(memory_space=pltpu.HBM)


def keep_in_hbm(array):
    return pltpu.with_memory_space_constraint(array, pltpu.HBM)


def my_freq():
    return lax.axis_index("core") * 2 + lax.axis_index("xl")


def split(value):
    high = value.astype(jnp.bfloat16)
    low = (value - high.astype(jnp.float32)).astype(jnp.bfloat16)
    return high, low


def swap_pairs(value):
    count = value.shape[0]
    up = pltpu.roll(value, count - 1, 0)
    down = pltpu.roll(value, 1, 0)
    row = lax.broadcasted_iota(jnp.int32, value.shape, 0)
    return jnp.where(row % 2 == 0, up, -down)


def replica_kernel(pos_hbm, cand_hbm, wave_hbm, held_ref, rest_hbm, scale_ref, pos_ref, cand_ref, wave_ref, rest_ref, sem):
    pairs = ((pos_hbm, pos_ref), (cand_hbm, cand_ref), (wave_hbm, wave_ref))
    loads = [pltpu.make_async_copy(src, dst, sem.at[n]) for n, (src, dst) in enumerate(pairs)]
    for load in loads:
        load.start()
    for load in loads:
        load.wait()
    freq, zh = my_freq(), lax.axis_index("zh")
    turn = wave_ref[freq] * (0.5 / np.pi)
    cx, cz2 = [], []
    for xl in range(2):
        lanes = pl.ds(pl.multiple_of((xl * 4 + zh) * LANES, LANES), LANES)
        grids = cand_ref[:, lanes]
        bin_of = lax.broadcasted_iota(jnp.int32, grids.shape, 0)
        grid = jnp.sum(jnp.where(bin_of == freq, grids, 0), axis=0, keepdims=True)
        cx.append(((grid % GRID_SIDE).astype(jnp.float32) - GRID_SIDE / 2) * 8.0)
        depth = 50.0 + (grid // GRID_SIDE).astype(jnp.float32) * 4.0
        cz2.append(depth * depth)

    def store(pair):
        return pltpu.make_async_copy(rest_ref.at[pair], rest_hbm.at[pair], sem.at[3])

    def pair_step(pair, out_ref, out_pair, norms):
        norms = list(norms)
        for half in range(2):
            lanes = pl.ds(pl.multiple_of(tile_of(pair * 2 + half) * LANES, LANES), LANES)
            px = jnp.broadcast_to(pos_ref[0:1, lanes], (LANES, LANES)).T
            py = pos_ref[1:2, lanes]
            py2 = jnp.broadcast_to(py * py, (LANES, LANES)).T
            for xl in range(2):
                for part in range(LANES // 32):
                    own = slice(part * 32, part * 32 + 32)
                    delta = px[own] - cx[xl]
                    r2 = delta * delta + (py2[own] + cz2[xl])
                    inv = lax.rsqrt(r2)
                    turns = (r2 * inv) * turn
                    x = turns - jnp.round(turns)
                    y = x * x
                    sin = x * series(SIN_C, y)
                    most = inv * sin
                    re_h, re_l = split(inv - most * sin)
                    im_h, im_l = split(most * series(COS_C, y))
                    rows = slice(half * LANES + part * 32, half * LANES + part * 32 + 32)
                    re = slice(xl * 2 * LANES, xl * 2 * LANES + LANES)
                    im = slice(xl * 2 * LANES + LANES, xl * 2 * LANES + 2 * LANES)
                    out_ref[out_pair, 0, rows, re] = re_h
                    out_ref[out_pair, 1, rows, re] = re_l
                    out_ref[out_pair, 0, rows, im] = im_h
                    out_ref[out_pair, 1, rows, im] = im_l
                    amp2 = inv * inv
                    norms[xl] += (amp2[0:8] + amp2[8:16]) + (amp2[16:24] + amp2[24:32])
        return tuple(norms)

    def rest_step(pair, norms):
        norms = pair_step(pair + HELD, rest_ref, pair, norms)
        store(pair).start()
        return norms

    norms = (jnp.zeros((8, LANES), jnp.float32),) * 2
    norms = lax.fori_loop(0, PAIRS - HELD, rest_step, norms, unroll=UNROLL)
    norms = lax.fori_loop(0, HELD, lambda pair, norms: pair_step(pair, held_ref, pair, norms), norms, unroll=UNROLL)
    for xl in range(2):
        norm = jnp.sum(norms[xl], axis=0, keepdims=True)
        scale_ref[xl] = jnp.broadcast_to(1.0 / (WINDOWS * norm), (8, LANES))

    @pl.loop(0, PAIRS - HELD)
    def _(pair):
        store(pair).wait()


def make_replicas(positions, cands, wavenumbers):
    held = jax.ShapeDtypeStruct((HELD, 2, 2 * LANES, 4 * LANES), jnp.bfloat16)
    rest = pltpu.HBM((PAIRS - HELD, 2, 2 * LANES, 4 * LANES), jnp.bfloat16)
    return pl.pallas_call(
        replica_kernel,
        out_shape=(held, rest, jax.ShapeDtypeStruct((2, 8, LANES), jnp.float32)),
        in_specs=[in_hbm()] * 3,
        out_specs=(in_vmem(), in_hbm(), in_vmem()),
        scratch_shapes=[
            pltpu.VMEM(positions.shape, jnp.float32),
            pltpu.VMEM(cands.shape, jnp.int32),
            pltpu.SMEM(wavenumbers.shape, jnp.float32),
            pltpu.VMEM(rest.shape, jnp.bfloat16),
            pltpu.SemaphoreType.DMA((4,)),
        ],
        compiler_params=pltpu.CompilerParams(vmem_limit_bytes=VMEM_LIMIT),
        cost_estimate=pl.CostEstimate(flops=60_000_000, bytes_accessed=10_000_000, transcendentals=1_000_000),
        name="replicas",
    )(*[keep_in_hbm(array) for array in (positions, cands, wavenumbers)])


def message_kernel(order_ref, spec_ref, held_ref, rest_hbm, scale_ref, out_ref, ordered, rest_ref, sem):
    zh = lax.axis_index("zh")
    loads = [pltpu.make_async_copy(rest_hbm.at[n], rest_ref.at[n], sem.at[n]) for n in range(PAIRS - HELD)]
    for load in loads:
        load.start()
    proj = jnp.zeros((ROWS, 4 * LANES), jnp.float32)
    for some in range(SEGS // 4):
        for seg in range(some * 4, some * 4 + 4):
            index = jnp.broadcast_to(order_ref[seg:seg + 1, :], (8, LANES))
            lane = index % LANES
            home = index // LANES
            total = [jnp.zeros((8, LANES), jnp.float32) for _ in range(ROWS // 8)]
            for run in range(SEGS):
                here = home == tile_of(run)
                for part in range(ROWS // 8):
                    there = jnp.take_along_axis(spec_ref[run, part * 8:part * 8 + 8, :], lane, axis=1)
                    total[part] = jnp.where(here, there, total[part])
            for part in range(ROWS // 8):
                ordered[seg, part * 8:part * 8 + 8, :] = total[part]
        for pair in range(some * 2, some * 2 + 2):
            data = jnp.concatenate([spec_ref[pair * 2], spec_ref[pair * 2 + 1]], axis=1)
            data_h, data_l = split(data)
            both = jnp.concatenate([data_h, data_l], axis=0)
            if pair < HELD:
                high, low = held_ref[pair, 0], held_ref[pair, 1]
            else:
                loads[pair - HELD].wait()
                high, low = rest_ref[pair - HELD, 0], rest_ref[pair - HELD, 1]
            first = jnp.dot(both, high, preferred_element_type=jnp.float32)
            second = jnp.dot(data_h, low, preferred_element_type=jnp.float32)
            proj += first[:ROWS] + first[ROWS:] + second

    powers = []
    for xl in range(2):
        real = proj[:, xl * 2 * LANES:xl * 2 * LANES + LANES]
        value = real + swap_pairs(proj[:, xl * 2 * LANES + LANES:xl * 2 * LANES + 2 * LANES])
        powers.append(jnp.sum(value * value, axis=0, keepdims=True) * scale_ref[xl, 0:1, :])
    for peer, (y, xl, xh, zl, core) in enumerate(PEER):
        start = peer * MSG
        out_ref[start:start + ROWS, :] = ordered[xl * 16 + zh * 4 + zl * 2 + core]
        for run in range(2):
            place = slice(start + (1 + run) * ROWS, start + (2 + run) * ROWS)
            out_ref[place, :] = ordered[(y * 2 + xh) * 4 + core * 2 + run]
        out_ref[start + 3 * ROWS:start + MSG, :] = jnp.broadcast_to(powers[xl], (MSG - 3 * ROWS, LANES))


def make_messages(order, spec, held, rest, scale):
    return pl.pallas_call(
        message_kernel,
        out_shape=jax.ShapeDtypeStruct((PEERS * MSG, LANES), jnp.float32),
        in_specs=[in_vmem(), in_vmem(), in_vmem(), in_hbm(), in_vmem()],
        out_specs=in_vmem(),
        scratch_shapes=[
            pltpu.VMEM((SEGS, ROWS, LANES), jnp.float32),
            pltpu.VMEM(rest.shape, rest.dtype),
            pltpu.SemaphoreType.DMA((PAIRS - HELD,)),
        ],
        compiler_params=pltpu.CompilerParams(vmem_limit_bytes=VMEM_LIMIT),
        cost_estimate=pl.CostEstimate(flops=100_000_000, bytes_accessed=10_000_000, transcendentals=0),
        name="messages",
    )(order, spec, held, keep_in_hbm(rest), scale)


def gather_rows(ref, freq, start):
    each = ref.shape[0] // PEERS
    return jnp.concatenate([ref[n * each + start:n * each + start + ROWS, :] for n in HOLDERS[freq]], axis=0)


def product(left_h, left_l, ref, freq, start):
    parts = [gather_rows(ref, freq, start + run * ROWS) for run in range(2)]
    right_h, right_l = split(jnp.concatenate(parts, axis=1))
    total = jnp.dot(left_h, right_h, preferred_element_type=jnp.float32)
    total += jnp.dot(left_h, right_l, preferred_element_type=jnp.float32)
    return total + jnp.dot(left_l, right_h, preferred_element_type=jnp.float32)


def send_out(freq, half, total, stage, out_ref, sem):
    stage[freq, 0] = total[:LANES]
    stage[freq, 1] = total[LANES:]
    columns = pl.ds(pl.multiple_of(half * 2 * LANES, 2 * LANES), 2 * LANES)
    copy = pltpu.make_async_copy(stage.at[freq], out_ref.at[freq, :, :, columns], sem.at[freq])
    copy.start()
    return copy


def column_kernel(got_ref, out_ref):
    for n in range(PEERS):
        out_ref[n * 2 * ROWS:(n + 1) * 2 * ROWS, :] = got_ref[n * MSG + ROWS:n * MSG + 3 * ROWS, :]


def take_columns(received):
    return pl.pallas_call(
        column_kernel,
        out_shape=jax.ShapeDtypeStruct((PEERS * 2 * ROWS, LANES), jnp.float32),
        in_specs=[in_vmem()],
        out_specs=in_vmem(),
        compiler_params=pltpu.CompilerParams(vmem_limit_bytes=VMEM_LIMIT),
        name="columns",
    )(received)


def own_density_kernel(got_ref, out_ref, high_ref, low_ref, beam_ref, stage, sem):
    mine = (lax.axis_index(("zl", "core")) * 8 + lax.axis_index(WIN)) * 4
    for freq in range(4):
        shares = [got_ref[n * MSG + 3 * ROWS:n * MSG + 3 * ROWS + 1, :] for n in HOLDERS[freq]]
        while len(shares) > 1:
            shares = [a + b for a, b in zip(shares[::2], shares[1::2])]
        beam_ref[freq:freq + 1, :] = pltpu.roll(shares[0], lax.rem(LANES - mine, LANES), 1)[:, 0:4]
    copies = []
    for freq in range(4):
        rows = gather_rows(got_ref, freq, 0) * (1.0 / WINDOWS)
        left = jnp.concatenate([rows, swap_pairs(rows)], axis=1)
        left_h, left_l = split(left.T)
        high_ref[freq] = left_h
        low_ref[freq] = left_l
        total = product(left_h, left_l, got_ref, freq, ROWS)
        copies.append(send_out(freq, lax.axis_index("core"), total, stage, out_ref, sem))
    for copy in copies:
        copy.wait()


def other_density_kernel(high_ref, low_ref, got_ref, base_ref, out_ref, stage, sem):
    del base_ref
    copies = []
    for freq in range(4):
        total = product(high_ref[freq], low_ref[freq], got_ref, freq, 0)
        copies.append(send_out(freq, 1 - lax.axis_index("core"), total, stage, out_ref, sem))
    for copy in copies:
        copy.wait()


def make_density(received):
    density = jax.ShapeDtypeStruct((4, 2, LANES, 4 * LANES), jnp.float32)
    left = jax.ShapeDtypeStruct((4, 2 * LANES, 2 * LANES), jnp.bfloat16)
    scratch = [pltpu.VMEM((4, 2, LANES, 2 * LANES), jnp.float32), pltpu.SemaphoreType.DMA((4,))]
    params = pltpu.CompilerParams(vmem_limit_bytes=VMEM_LIMIT)
    cost = pl.CostEstimate(flops=800_000_000, bytes_accessed=5_000_000, transcendentals=0)
    anywhere = in_hbm()
    half, high, low, beam = pl.pallas_call(
        own_density_kernel,
        out_shape=(density, left, left, jax.ShapeDtypeStruct((4, 4), jnp.float32)),
        in_specs=[in_vmem()],
        out_specs=(anywhere, in_vmem(), in_vmem(), in_vmem()),
        scratch_shapes=scratch,
        compiler_params=params,
        cost_estimate=cost,
        name="own_density",
    )(received)
    other = lax.ppermute(take_columns(received), "core", [(0, 1), (1, 0)])
    density = pl.pallas_call(
        other_density_kernel,
        out_shape=density,
        in_specs=[in_vmem(), in_vmem(), in_vmem(), anywhere],
        out_specs=anywhere,
        scratch_shapes=scratch,
        input_output_aliases={3: 0},
        compiler_params=params,
        cost_estimate=cost,
        name="other_density",
    )(high, low, other, half)
    return density, beam


def local(spectra, sensor_positions, wavenumbers, sensor_order, candidates):
    parts = spectra.reshape(2, 2, 1, 2, ROWS, LANES)
    outgoing = jnp.broadcast_to(parts, (2, 2, 4, 2, ROWS, LANES))
    gathered = lax.all_to_all(outgoing.reshape(SEGS, ROWS, LANES), GATHER, 0, 0, tiled=True)
    held, rest, scale = make_replicas(sensor_positions, candidates, wavenumbers)
    messages = make_messages(sensor_order.reshape(SEGS, LANES), gathered, held, rest, scale)
    received = lax.all_to_all(messages.reshape(PEERS, MSG // 2, 2, LANES), SPREAD, 0, 0, tiled=True)
    return make_density(received.reshape(PEERS * MSG, LANES))


def solution(mesh):
    fine = Mesh(mesh.devices.reshape(SIZES), NAMES)
    in_specs = (P(None, WIN, None, TILE), P(), P(), P(), P())
    out_specs = (P(None, None, TILE, WIN), P(None, TILE + WIN))
    return jax.shard_map(local, mesh=fine, in_specs=in_specs, out_specs=out_specs, check_vma=False)
```

```python
import jax
import jax.numpy as jnp
import numpy as np
from jax import lax
from jax.experimental import pallas as pl
from jax.experimental.pallas import tpu as pltpu
from jax.sharding import Mesh, PartitionSpec as P

GRID_SIDE = 64
WINDOWS = 128
LANES = 128
SEGS = 32
ROWS = 16
PEERS = 64
MSG = 3 * ROWS + 1
VMEM_LIMIT = 24 * 1024 * 1024
UNROLL = 4
PAIRS = SEGS // 2
HELD = 6
NAMES = ("xl", "zh", "zl", "core", "y", "xh")
SIZES = (2, 4, 2, 2, 4, 2)
TILE = ("xl", "zh", "zl", "core")
WIN = ("y", "xh")
GATHER = ("core", "xl", "zh", "zl")
SPREAD = ("y", "xl", "xh", "zl", "core")

PEER = [(y, xl, xh, zl, core) for y in range(4) for xl in range(2) for xh in range(2) for zl in range(2) for core in range(2)]
HOLDERS = [[n for n, p in enumerate(PEER) if p[4] * 2 + p[1] == freq] for freq in range(4)]


def tile_of(run):
    return (run % 16) * 2 + run // 16


def half_turn_series():
    x = np.cos(np.linspace(0.0, np.pi, 4001)) * 0.5
    y = x * x
    powers = y[:, None] ** np.arange(5)[None, :]
    sin_c = np.linalg.lstsq(powers[:, :5], np.sqrt(2.0) * np.pi * np.sinc(x), rcond=None)[0]
    cos_c = np.linalg.lstsq(powers[:, :5], -np.sqrt(2.0) * np.cos(np.pi * x), rcond=None)[0]
    return [float(v) for v in sin_c], [float(v) for v in cos_c]


SIN_C, COS_C = half_turn_series()


def series(coefficients, y):
    total = coefficients[-1] * y + coefficients[-2]
    for c in coefficients[-3::-1]:
        total = total * y + c
    return total


def in_vmem():
    return pl.BlockSpec(memory_space=pltpu.VMEM)


def in_hbm():
    return pl.BlockSpec(memory_space=pltpu.HBM)


def keep_in_hbm(array):
    return pltpu.with_memory_space_constraint(array, pltpu.HBM)


def my_freq():
    return lax.axis_index("core") * 2 + lax.axis_index("xl")


def split(value):
    high = value.astype(jnp.bfloat16)
    low = (value - high.astype(jnp.float32)).astype(jnp.bfloat16)
    return high, low


def swap_pairs(value):
    count = value.shape[0]
    up = pltpu.roll(value, count - 1, 0)
    down = pltpu.roll(value, 1, 0)
    row = lax.broadcasted_iota(jnp.int32, value.shape, 0)
    return jnp.where(row % 2 == 0, up, -down)


def replica_kernel(pos_hbm, cand_hbm, wave_hbm, held_ref, rest_hbm, scale_ref, pos_ref, cand_ref, wave_ref, rest_ref, sem):
    pairs = ((pos_hbm, pos_ref), (cand_hbm, cand_ref), (wave_hbm, wave_ref))
    loads = [pltpu.make_async_copy(src, dst, sem.at[n]) for n, (src, dst) in enumerate(pairs)]
    for load in loads:
        load.start()
    for load in loads:
        load.wait()
    freq, zh = my_freq(), lax.axis_index("zh")
    turn = wave_ref[freq] * (0.5 / np.pi)
    cx, cz2 = [], []
    for xl in range(2):
        lanes = pl.ds(pl.multiple_of((xl * 4 + zh) * LANES, LANES), LANES)
        grids = cand_ref[:, lanes]
        bin_of = lax.broadcasted_iota(jnp.int32, grids.shape, 0)
        grid = jnp.sum(jnp.where(bin_of == freq, grids, 0), axis=0, keepdims=True)
        cx.append(((grid % GRID_SIDE).astype(jnp.float32) - GRID_SIDE / 2) * 8.0)
        depth = 50.0 + (grid // GRID_SIDE).astype(jnp.float32) * 4.0
        cz2.append(depth * depth)

    def store(pair):
        return pltpu.make_async_copy(rest_ref.at[pair], rest_hbm.at[pair], sem.at[3])

    def pair_step(pair, out_ref, out_pair, norms):
        norms = list(norms)
        for half in range(2):
            lanes = pl.ds(pl.multiple_of(tile_of(pair * 2 + half) * LANES, LANES), LANES)
            px = jnp.broadcast_to(pos_ref[0:1, lanes], (LANES, LANES)).T
            py = pos_ref[1:2, lanes]
            py2 = jnp.broadcast_to(py * py, (LANES, LANES)).T
            for xl in range(2):
                for part in range(LANES // 32):
                    own = slice(part * 32, part * 32 + 32)
                    delta = px[own] - cx[xl]
                    r2 = delta * delta + (py2[own] + cz2[xl])
                    inv = lax.rsqrt(r2)
                    turns = (r2 * inv) * turn
                    x = turns - jnp.round(turns)
                    y = x * x
                    sin = x * series(SIN_C, y)
                    most = inv * sin
                    re_h, re_l = split(inv - most * sin)
                    im_h, im_l = split(most * series(COS_C, y))
                    rows = slice(half * LANES + part * 32, half * LANES + part * 32 + 32)
                    re = slice(xl * 2 * LANES, xl * 2 * LANES + LANES)
                    im = slice(xl * 2 * LANES + LANES, xl * 2 * LANES + 2 * LANES)
                    out_ref[out_pair, 0, rows, re] = re_h
                    out_ref[out_pair, 1, rows, re] = re_l
                    out_ref[out_pair, 0, rows, im] = im_h
                    out_ref[out_pair, 1, rows, im] = im_l
                    amp2 = inv * inv
                    norms[xl] += (amp2[0:8] + amp2[8:16]) + (amp2[16:24] + amp2[24:32])
        return tuple(norms)

    def rest_step(pair, norms):
        norms = pair_step(pair + HELD, rest_ref, pair, norms)
        store(pair).start()
        return norms

    norms = (jnp.zeros((8, LANES), jnp.float32),) * 2
    norms = lax.fori_loop(0, PAIRS - HELD, rest_step, norms, unroll=UNROLL)
    norms = lax.fori_loop(0, HELD, lambda pair, norms: pair_step(pair, held_ref, pair, norms), norms, unroll=UNROLL)
    for xl in range(2):
        norm = jnp.sum(norms[xl], axis=0, keepdims=True)
        scale_ref[xl] = jnp.broadcast_to(1.0 / (WINDOWS * norm), (8, LANES))

    @pl.loop(0, PAIRS - HELD)
    def _(pair):
        store(pair).wait()


def make_replicas(positions, cands, wavenumbers):
    held = jax.ShapeDtypeStruct((HELD, 2, 2 * LANES, 4 * LANES), jnp.bfloat16)
    rest = pltpu.HBM((PAIRS - HELD, 2, 2 * LANES, 4 * LANES), jnp.bfloat16)
    return pl.pallas_call(
        replica_kernel,
        out_shape=(held, rest, jax.ShapeDtypeStruct((2, 8, LANES), jnp.float32)),
        in_specs=[in_hbm()] * 3,
        out_specs=(in_vmem(), in_hbm(), in_vmem()),
        scratch_shapes=[
            pltpu.VMEM(positions.shape, jnp.float32),
            pltpu.VMEM(cands.shape, jnp.int32),
            pltpu.SMEM(wavenumbers.shape, jnp.float32),
            pltpu.VMEM(rest.shape, jnp.bfloat16),
            pltpu.SemaphoreType.DMA((4,)),
        ],
        compiler_params=pltpu.CompilerParams(vmem_limit_bytes=VMEM_LIMIT),
        cost_estimate=pl.CostEstimate(flops=60_000_000, bytes_accessed=10_000_000, transcendentals=1_000_000),
        name="replicas",
    )(*[keep_in_hbm(array) for array in (positions, cands, wavenumbers)])


def message_kernel(order_ref, spec_ref, held_ref, rest_hbm, scale_ref, out_ref, ordered, rest_ref, sem):
    zh = lax.axis_index("zh")
    loads = [pltpu.make_async_copy(rest_hbm.at[n], rest_ref.at[n], sem.at[n]) for n in range(PAIRS - HELD)]
    for load in loads:
        load.start()
    proj = jnp.zeros((ROWS, 4 * LANES), jnp.float32)
    for some in range(SEGS // 4):
        for seg in range(some * 4, some * 4 + 4):
            index = jnp.broadcast_to(order_ref[seg:seg + 1, :], (8, LANES))
            lane = index % LANES
            home = index // LANES
            total = [jnp.zeros((8, LANES), jnp.float32) for _ in range(ROWS // 8)]
            for run in range(SEGS):
                here = home == tile_of(run)
                for part in range(ROWS // 8):
                    there = jnp.take_along_axis(spec_ref[run, part * 8:part * 8 + 8, :], lane, axis=1)
                    total[part] = jnp.where(here, there, total[part])
            for part in range(ROWS // 8):
                ordered[seg, part * 8:part * 8 + 8, :] = total[part]
        for pair in range(some * 2, some * 2 + 2):
            data = jnp.concatenate([spec_ref[pair * 2], spec_ref[pair * 2 + 1]], axis=1)
            data_h, data_l = split(data)
            both = jnp.concatenate([data_h, data_l], axis=0)
            if pair < HELD:
                high, low = held_ref[pair, 0], held_ref[pair, 1]
            else:
                loads[pair - HELD].wait()
                high, low = rest_ref[pair - HELD, 0], rest_ref[pair - HELD, 1]
            first = jnp.dot(both, high, preferred_element_type=jnp.float32)
            second = jnp.dot(data_h, low, preferred_element_type=jnp.float32)
            proj += first[:ROWS] + first[ROWS:] + second

    powers = []
    for xl in range(2):
        real = proj[:, xl * 2 * LANES:xl * 2 * LANES + LANES]
        value = real + swap_pairs(proj[:, xl * 2 * LANES + LANES:xl * 2 * LANES + 2 * LANES])
        powers.append(jnp.sum(value * value, axis=0, keepdims=True) * scale_ref[xl, 0:1, :])
    for peer, (y, xl, xh, zl, core) in enumerate(PEER):
        start = peer * MSG
        out_ref[start:start + ROWS, :] = ordered[xl * 16 + zh * 4 + zl * 2 + core]
        for run in range(2):
            place = slice(start + (1 + run) * ROWS, start + (2 + run) * ROWS)
            out_ref[place, :] = ordered[(y * 2 + xh) * 4 + core * 2 + run]
        out_ref[start + 3 * ROWS:start + MSG, :] = jnp.broadcast_to(powers[xl], (MSG - 3 * ROWS, LANES))


def make_messages(order, spec, held, rest, scale):
    return pl.pallas_call(
        message_kernel,
        out_shape=jax.ShapeDtypeStruct((PEERS * MSG, LANES), jnp.float32),
        in_specs=[in_vmem(), in_vmem(), in_vmem(), in_hbm(), in_vmem()],
        out_specs=in_vmem(),
        scratch_shapes=[
            pltpu.VMEM((SEGS, ROWS, LANES), jnp.float32),
            pltpu.VMEM(rest.shape, rest.dtype),
            pltpu.SemaphoreType.DMA((PAIRS - HELD,)),
        ],
        compiler_params=pltpu.CompilerParams(vmem_limit_bytes=VMEM_LIMIT),
        cost_estimate=pl.CostEstimate(flops=100_000_000, bytes_accessed=10_000_000, transcendentals=0),
        name="messages",
    )(order, spec, held, keep_in_hbm(rest), scale)


def gather_rows(ref, freq, start):
    each = ref.shape[0] // PEERS
    return jnp.concatenate([ref[n * each + start:n * each + start + ROWS, :] for n in HOLDERS[freq]], axis=0)


def product(left_h, left_l, ref, freq, start):
    parts = [gather_rows(ref, freq, start + run * ROWS) for run in range(2)]
    right_h, right_l = split(jnp.concatenate(parts, axis=1))
    total = jnp.dot(left_h, right_h, preferred_element_type=jnp.float32)
    total += jnp.dot(left_h, right_l, preferred_element_type=jnp.float32)
    return total + jnp.dot(left_l, right_h, preferred_element_type=jnp.float32)


def send_out(freq, half, total, stage, out_ref, sem):
    stage[freq, 0] = total[:LANES]
    stage[freq, 1] = total[LANES:]
    columns = pl.ds(pl.multiple_of(half * 2 * LANES, 2 * LANES), 2 * LANES)
    copy = pltpu.make_async_copy(stage.at[freq], out_ref.at[freq, :, :, columns], sem.at[freq])
    copy.start()
    return copy


def column_kernel(got_ref, out_ref):
    for n in range(PEERS):
        out_ref[n * 2 * ROWS:(n + 1) * 2 * ROWS, :] = got_ref[n * MSG + ROWS:n * MSG + 3 * ROWS, :]


def take_columns(received):
    return pl.pallas_call(
        column_kernel,
        out_shape=jax.ShapeDtypeStruct((PEERS * 2 * ROWS, LANES), jnp.float32),
        in_specs=[in_vmem()],
        out_specs=in_vmem(),
        compiler_params=pltpu.CompilerParams(vmem_limit_bytes=VMEM_LIMIT),
        name="columns",
    )(received)


def own_density_kernel(got_ref, out_ref, high_ref, low_ref, beam_ref, stage, sem):
    mine = (lax.axis_index(("zl", "core")) * 8 + lax.axis_index(WIN)) * 4
    for freq in range(4):
        shares = [got_ref[n * MSG + 3 * ROWS:n * MSG + 3 * ROWS + 1, :] for n in HOLDERS[freq]]
        while len(shares) > 1:
            shares = [a + b for a, b in zip(shares[::2], shares[1::2])]
        beam_ref[freq:freq + 1, :] = pltpu.roll(shares[0], lax.rem(LANES - mine, LANES), 1)[:, 0:4]
    copies = []
    for freq in range(4):
        rows = gather_rows(got_ref, freq, 0) * (1.0 / WINDOWS)
        left = jnp.concatenate([rows, swap_pairs(rows)], axis=1)
        left_h, left_l = split(left.T)
        high_ref[freq] = left_h
        low_ref[freq] = left_l
        total = product(left_h, left_l, got_ref, freq, ROWS)
        copies.append(send_out(freq, lax.axis_index("core"), total, stage, out_ref, sem))
    for copy in copies:
        copy.wait()


def other_density_kernel(high_ref, low_ref, got_ref, base_ref, out_ref, stage, sem):
    del base_ref
    copies = []
    for freq in range(4):
        total = product(high_ref[freq], low_ref[freq], got_ref, freq, 0)
        copies.append(send_out(freq, 1 - lax.axis_index("core"), total, stage, out_ref, sem))
    for copy in copies:
        copy.wait()


def make_density(received):
    density = jax.ShapeDtypeStruct((4, 2, LANES, 4 * LANES), jnp.float32)
    left = jax.ShapeDtypeStruct((4, 2 * LANES, 2 * LANES), jnp.bfloat16)
    scratch = [pltpu.VMEM((4, 2, LANES, 2 * LANES), jnp.float32), pltpu.SemaphoreType.DMA((4,))]
    params = pltpu.CompilerParams(vmem_limit_bytes=VMEM_LIMIT)
    cost = pl.CostEstimate(flops=800_000_000, bytes_accessed=5_000_000, transcendentals=0)
    anywhere = in_hbm()
    half, high, low, beam = pl.pallas_call(
        own_density_kernel,
        out_shape=(density, left, left, jax.ShapeDtypeStruct((4, 4), jnp.float32)),
        in_specs=[in_vmem()],
        out_specs=(anywhere, in_vmem(), in_vmem(), in_vmem()),
        scratch_shapes=scratch,
        compiler_params=params,
        cost_estimate=cost,
        name="own_density",
    )(received)
    other = lax.ppermute(take_columns(received), "core", [(0, 1), (1, 0)])
    density = pl.pallas_call(
        other_density_kernel,
        out_shape=density,
        in_specs=[in_vmem(), in_vmem(), in_vmem(), anywhere],
        out_specs=anywhere,
        scratch_shapes=scratch,
        input_output_aliases={3: 0},
        compiler_params=params,
        cost_estimate=cost,
        name="other_density",
    )(high, low, other, half)
    return density, beam


def local(spectra, sensor_positions, wavenumbers, sensor_order, candidates):
    parts = spectra.reshape(2, 2, 1, 2, ROWS, LANES)
    outgoing = jnp.broadcast_to(parts, (2, 2, 4, 2, ROWS, LANES))
    gathered = lax.all_to_all(outgoing.reshape(SEGS, ROWS, LANES), GATHER, 0, 0, tiled=True)
    held, rest, scale = make_replicas(sensor_positions, candidates, wavenumbers)
    messages = make_messages(sensor_order.reshape(SEGS, LANES), gathered, held, rest, scale)
    received = lax.all_to_all(messages.reshape(PEERS, MSG, 1, LANES), SPREAD, 0, 0, tiled=True)
    return make_density(received.reshape(PEERS * MSG, LANES))


def solution(mesh):
    fine = Mesh(mesh.devices.reshape(SIZES), NAMES)
    in_specs = (P(None, WIN, None, TILE), P(), P(), P(), P())
    out_specs = (P(None, None, TILE, WIN), P(None, TILE + WIN))
    return jax.shard_map(local, mesh=fine, in_specs=in_specs, out_specs=out_specs, check_vma=False)
```

```python
import jax
import jax.numpy as jnp
import numpy as np
from jax import lax
from jax.experimental import pallas as pl
from jax.experimental.pallas import tpu as pltpu
from jax.sharding import Mesh, PartitionSpec as P

GRID_SIDE = 64
WINDOWS = 128
LANES = 128
SEGS = 32
ROWS = 16
PEERS = 64
MSG = 3 * ROWS + 1
VMEM_LIMIT = 24 * 1024 * 1024
UNROLL = 4
PAIRS = SEGS // 2
HELD = 6
NAMES = ("xl", "zh", "zl", "core", "y", "xh")
SIZES = (2, 4, 2, 2, 4, 2)
TILE = ("xl", "zh", "zl", "core")
WIN = ("y", "xh")
GATHER = ("core", "xl", "zh", "zl")
SPREAD = ("y", "xl", "xh", "zl", "core")

PEER = [(y, xl, xh, zl, core) for y in range(4) for xl in range(2) for xh in range(2) for zl in range(2) for core in range(2)]
HOLDERS = [[n for n, p in enumerate(PEER) if p[4] * 2 + p[1] == freq] for freq in range(4)]


def tile_of(run):
    return (run % 16) * 2 + run // 16


def half_turn_series():
    x = np.cos(np.linspace(0.0, np.pi, 4001)) * 0.5
    y = x * x
    powers = y[:, None] ** np.arange(5)[None, :]
    sin_c = np.linalg.lstsq(powers[:, :5], np.sqrt(2.0) * np.pi * np.sinc(x), rcond=None)[0]
    cos_c = np.linalg.lstsq(powers[:, :5], -np.sqrt(2.0) * np.cos(np.pi * x), rcond=None)[0]
    return [float(v) for v in sin_c], [float(v) for v in cos_c]


SIN_C, COS_C = half_turn_series()


def series(coefficients, y):
    total = coefficients[-1] * y + coefficients[-2]
    for c in coefficients[-3::-1]:
        total = total * y + c
    return total


def in_vmem():
    return pl.BlockSpec(memory_space=pltpu.VMEM)


def in_hbm():
    return pl.BlockSpec(memory_space=pltpu.HBM)


def keep_in_hbm(array):
    return pltpu.with_memory_space_constraint(array, pltpu.HBM)


def my_freq():
    return lax.axis_index("core") * 2 + lax.axis_index("xl")


def split(value):
    high = value.astype(jnp.bfloat16)
    low = (value - high.astype(jnp.float32)).astype(jnp.bfloat16)
    return high, low


def swap_pairs(value):
    count = value.shape[0]
    up = pltpu.roll(value, count - 1, 0)
    down = pltpu.roll(value, 1, 0)
    row = lax.broadcasted_iota(jnp.int32, value.shape, 0)
    return jnp.where(row % 2 == 0, up, -down)


def replica_kernel(pos_hbm, cand_hbm, wave_hbm, held_ref, rest_hbm, scale_ref, pos_ref, cand_ref, wave_ref, rest_ref, sem):
    pairs = ((pos_hbm, pos_ref), (cand_hbm, cand_ref), (wave_hbm, wave_ref))
    loads = [pltpu.make_async_copy(src, dst, sem.at[n]) for n, (src, dst) in enumerate(pairs)]
    for load in loads:
        load.start()
    for load in loads:
        load.wait()
    freq, zh = my_freq(), lax.axis_index("zh")
    turn = wave_ref[freq] * (0.5 / np.pi)
    cx, cz2 = [], []
    for xl in range(2):
        lanes = pl.ds(pl.multiple_of((xl * 4 + zh) * LANES, LANES), LANES)
        grids = cand_ref[:, lanes]
        bin_of = lax.broadcasted_iota(jnp.int32, grids.shape, 0)
        grid = jnp.sum(jnp.where(bin_of == freq, grids, 0), axis=0, keepdims=True)
        cx.append(((grid % GRID_SIDE).astype(jnp.float32) - GRID_SIDE / 2) * 8.0)
        depth = 50.0 + (grid // GRID_SIDE).astype(jnp.float32) * 4.0
        cz2.append(depth * depth)

    def store(pair):
        return pltpu.make_async_copy(rest_ref.at[pair], rest_hbm.at[pair], sem.at[3])

    def pair_step(pair, out_ref, out_pair, norms):
        norms = list(norms)
        for half in range(2):
            lanes = pl.ds(pl.multiple_of(tile_of(pair * 2 + half) * LANES, LANES), LANES)
            px = jnp.broadcast_to(pos_ref[0:1, lanes], (LANES, LANES)).T
            py = pos_ref[1:2, lanes]
            py2 = jnp.broadcast_to(py * py, (LANES, LANES)).T
            for xl in range(2):
                for part in range(LANES // 32):
                    own = slice(part * 32, part * 32 + 32)
                    delta = px[own] - cx[xl]
                    r2 = delta * delta + (py2[own] + cz2[xl])
                    inv = lax.rsqrt(r2)
                    turns = (r2 * inv) * turn
                    x = turns - jnp.round(turns)
                    y = x * x
                    sin = x * series(SIN_C, y)
                    most = inv * sin
                    re_h, re_l = split(inv - most * sin)
                    im_h, im_l = split(most * series(COS_C, y))
                    rows = slice(half * LANES + part * 32, half * LANES + part * 32 + 32)
                    re = slice(xl * 2 * LANES, xl * 2 * LANES + LANES)
                    im = slice(xl * 2 * LANES + LANES, xl * 2 * LANES + 2 * LANES)
                    out_ref[out_pair, 0, rows, re] = re_h
                    out_ref[out_pair, 1, rows, re] = re_l
                    out_ref[out_pair, 0, rows, im] = im_h
                    out_ref[out_pair, 1, rows, im] = im_l
                    amp2 = inv * inv
                    norms[xl] += (amp2[0:8] + amp2[8:16]) + (amp2[16:24] + amp2[24:32])
        return tuple(norms)

    def rest_step(pair, norms):
        norms = pair_step(pair + HELD, rest_ref, pair, norms)
        store(pair).start()
        return norms

    norms = (jnp.zeros((8, LANES), jnp.float32),) * 2
    norms = lax.fori_loop(0, PAIRS - HELD, rest_step, norms, unroll=UNROLL)
    norms = lax.fori_loop(0, HELD, lambda pair, norms: pair_step(pair, held_ref, pair, norms), norms, unroll=UNROLL)
    for xl in range(2):
        norm = jnp.sum(norms[xl], axis=0, keepdims=True)
        scale_ref[xl] = jnp.broadcast_to(1.0 / (WINDOWS * norm), (8, LANES))

    @pl.loop(0, PAIRS - HELD)
    def _(pair):
        store(pair).wait()


def make_replicas(positions, cands, wavenumbers):
    held = jax.ShapeDtypeStruct((HELD, 2, 2 * LANES, 4 * LANES), jnp.bfloat16)
    rest = pltpu.HBM((PAIRS - HELD, 2, 2 * LANES, 4 * LANES), jnp.bfloat16)
    return pl.pallas_call(
        replica_kernel,
        out_shape=(held, rest, jax.ShapeDtypeStruct((2, 8, LANES), jnp.float32)),
        in_specs=[in_hbm()] * 3,
        out_specs=(in_vmem(), in_hbm(), in_vmem()),
        scratch_shapes=[
            pltpu.VMEM(positions.shape, jnp.float32),
            pltpu.VMEM(cands.shape, jnp.int32),
            pltpu.SMEM(wavenumbers.shape, jnp.float32),
            pltpu.VMEM(rest.shape, jnp.bfloat16),
            pltpu.SemaphoreType.DMA((4,)),
        ],
        compiler_params=pltpu.CompilerParams(vmem_limit_bytes=VMEM_LIMIT),
        cost_estimate=pl.CostEstimate(flops=60_000_000, bytes_accessed=10_000_000, transcendentals=1_000_000),
        name="replicas",
    )(*[keep_in_hbm(array) for array in (positions, cands, wavenumbers)])


def message_kernel(order_ref, spec_ref, held_ref, rest_hbm, scale_ref, out_ref, ordered, rest_ref, sem):
    zh = lax.axis_index("zh")
    loads = [pltpu.make_async_copy(rest_hbm.at[n], rest_ref.at[n], sem.at[n]) for n in range(PAIRS - HELD)]
    for load in loads:
        load.start()
    proj = jnp.zeros((ROWS, 4 * LANES), jnp.float32)
    for some in range(SEGS // 4):
        for seg in range(some * 4, some * 4 + 4):
            index = jnp.broadcast_to(order_ref[seg:seg + 1, :], (8, LANES))
            lane = index % LANES
            home = index // LANES
            total = [jnp.zeros((8, LANES), jnp.float32) for _ in range(ROWS // 8)]
            for run in range(SEGS):
                here = home == tile_of(run)
                for part in range(ROWS // 8):
                    there = jnp.take_along_axis(spec_ref[run, part * 8:part * 8 + 8, :], lane, axis=1)
                    total[part] = jnp.where(here, there, total[part])
            for part in range(ROWS // 8):
                ordered[seg, part * 8:part * 8 + 8, :] = total[part]
        for pair in range(some * 2, some * 2 + 2):
            data = jnp.concatenate([spec_ref[pair * 2], spec_ref[pair * 2 + 1]], axis=1)
            data_h, data_l = split(data)
            both = jnp.concatenate([data_h, data_l], axis=0)
            if pair < HELD:
                high, low = held_ref[pair, 0], held_ref[pair, 1]
            else:
                loads[pair - HELD].wait()
                high, low = rest_ref[pair - HELD, 0], rest_ref[pair - HELD, 1]
            first = jnp.dot(both, high, preferred_element_type=jnp.float32)
            second = jnp.dot(data_h, low, preferred_element_type=jnp.float32)
            proj += first[:ROWS] + first[ROWS:] + second

    powers = []
    for xl in range(2):
        real = proj[:, xl * 2 * LANES:xl * 2 * LANES + LANES]
        value = real + swap_pairs(proj[:, xl * 2 * LANES + LANES:xl * 2 * LANES + 2 * LANES])
        powers.append(jnp.sum(value * value, axis=0, keepdims=True) * scale_ref[xl, 0:1, :])
    for peer, (y, xl, xh, zl, core) in enumerate(PEER):
        start = peer * MSG
        out_ref[start:start + ROWS, :] = ordered[xl * 16 + zh * 4 + zl * 2 + core]
        for run in range(2):
            place = slice(start + (1 + run) * ROWS, start + (2 + run) * ROWS)
            out_ref[place, :] = ordered[(y * 2 + xh) * 4 + core * 2 + run]
        out_ref[start + 3 * ROWS:start + MSG, :] = jnp.broadcast_to(powers[xl], (MSG - 3 * ROWS, LANES))


def make_messages(order, spec, held, rest, scale):
    return pl.pallas_call(
        message_kernel,
        out_shape=jax.ShapeDtypeStruct((PEERS * MSG, LANES), jnp.float32),
        in_specs=[in_vmem(), in_vmem(), in_vmem(), in_hbm(), in_vmem()],
        out_specs=in_vmem(),
        scratch_shapes=[
            pltpu.VMEM((SEGS, ROWS, LANES), jnp.float32),
            pltpu.VMEM(rest.shape, rest.dtype),
            pltpu.SemaphoreType.DMA((PAIRS - HELD,)),
        ],
        compiler_params=pltpu.CompilerParams(vmem_limit_bytes=VMEM_LIMIT),
        cost_estimate=pl.CostEstimate(flops=100_000_000, bytes_accessed=10_000_000, transcendentals=0),
        name="messages",
    )(order, spec, held, keep_in_hbm(rest), scale)


def gather_rows(ref, freq, start):
    each = ref.shape[0] // PEERS
    return jnp.concatenate([ref[n * each + start:n * each + start + ROWS, :] for n in HOLDERS[freq]], axis=0)


def product(left_h, left_l, ref, freq, start):
    parts = [gather_rows(ref, freq, start + run * ROWS) for run in range(2)]
    right_h, right_l = split(jnp.concatenate(parts, axis=1))
    total = jnp.dot(left_h, right_h, preferred_element_type=jnp.float32)
    total += jnp.dot(left_h, right_l, preferred_element_type=jnp.float32)
    return total + jnp.dot(left_l, right_h, preferred_element_type=jnp.float32)


def send_out(freq, half, total, stage, out_ref, sem):
    columns = pl.ds(pl.multiple_of(half * 2 * LANES, 2 * LANES), 2 * LANES)
    copies = []
    for part in range(2):
        stage[freq, part] = total[part * LANES:(part + 1) * LANES]
        copy = pltpu.make_async_copy(stage.at[freq, part], out_ref.at[freq, part, :, columns], sem.at[freq * 2 + part])
        copy.start()
        copies.append(copy)
    return copies


def column_kernel(got_ref, out_ref):
    for n in range(PEERS):
        out_ref[n * 2 * ROWS:(n + 1) * 2 * ROWS, :] = got_ref[n * MSG + ROWS:n * MSG + 3 * ROWS, :]


def take_columns(received):
    return pl.pallas_call(
        column_kernel,
        out_shape=jax.ShapeDtypeStruct((PEERS * 2 * ROWS, LANES), jnp.float32),
        in_specs=[in_vmem()],
        out_specs=in_vmem(),
        compiler_params=pltpu.CompilerParams(vmem_limit_bytes=VMEM_LIMIT),
        name="columns",
    )(received)


def own_density_kernel(got_ref, out_ref, high_ref, low_ref, beam_ref, stage, sem):
    mine = (lax.axis_index(("zl", "core")) * 8 + lax.axis_index(WIN)) * 4
    for freq in range(4):
        shares = [got_ref[n * MSG + 3 * ROWS:n * MSG + 3 * ROWS + 1, :] for n in HOLDERS[freq]]
        while len(shares) > 1:
            shares = [a + b for a, b in zip(shares[::2], shares[1::2])]
        beam_ref[freq:freq + 1, :] = pltpu.roll(shares[0], lax.rem(LANES - mine, LANES), 1)[:, 0:4]
    copies = []
    for freq in range(4):
        rows = gather_rows(got_ref, freq, 0) * (1.0 / WINDOWS)
        left = jnp.concatenate([rows, swap_pairs(rows)], axis=1)
        left_h, left_l = split(left.T)
        high_ref[freq] = left_h
        low_ref[freq] = left_l
        total = product(left_h, left_l, got_ref, freq, ROWS)
        copies.extend(send_out(freq, lax.axis_index("core"), total, stage, out_ref, sem))
    for copy in copies:
        copy.wait()


def other_density_kernel(high_ref, low_ref, got_ref, base_ref, out_ref, stage, sem):
    del base_ref
    copies = []
    for freq in range(4):
        total = product(high_ref[freq], low_ref[freq], got_ref, freq, 0)
        copies.extend(send_out(freq, 1 - lax.axis_index("core"), total, stage, out_ref, sem))
    for copy in copies:
        copy.wait()


def make_density(received):
    density = jax.ShapeDtypeStruct((4, 2, LANES, 4 * LANES), jnp.float32)
    left = jax.ShapeDtypeStruct((4, 2 * LANES, 2 * LANES), jnp.bfloat16)
    scratch = [pltpu.VMEM((4, 2, LANES, 2 * LANES), jnp.float32), pltpu.SemaphoreType.DMA((8,))]
    params = pltpu.CompilerParams(vmem_limit_bytes=VMEM_LIMIT)
    cost = pl.CostEstimate(flops=800_000_000, bytes_accessed=5_000_000, transcendentals=0)
    anywhere = in_hbm()
    half, high, low, beam = pl.pallas_call(
        own_density_kernel,
        out_shape=(density, left, left, jax.ShapeDtypeStruct((4, 4), jnp.float32)),
        in_specs=[in_vmem()],
        out_specs=(anywhere, in_vmem(), in_vmem(), in_vmem()),
        scratch_shapes=scratch,
        compiler_params=params,
        cost_estimate=cost,
        name="own_density",
    )(received)
    other = lax.ppermute(take_columns(received), "core", [(0, 1), (1, 0)])
    density = pl.pallas_call(
        other_density_kernel,
        out_shape=density,
        in_specs=[in_vmem(), in_vmem(), in_vmem(), anywhere],
        out_specs=anywhere,
        scratch_shapes=scratch,
        input_output_aliases={3: 0},
        compiler_params=params,
        cost_estimate=cost,
        name="other_density",
    )(high, low, other, half)
    return density, beam


def local(spectra, sensor_positions, wavenumbers, sensor_order, candidates):
    parts = spectra.reshape(2, 2, 1, 2, ROWS, LANES)
    outgoing = jnp.broadcast_to(parts, (2, 2, 4, 2, ROWS, LANES))
    gathered = lax.all_to_all(outgoing.reshape(SEGS, ROWS, LANES), GATHER, 0, 0, tiled=True)
    held, rest, scale = make_replicas(sensor_positions, candidates, wavenumbers)
    messages = make_messages(sensor_order.reshape(SEGS, LANES), gathered, held, rest, scale)
    received = lax.all_to_all(messages.reshape(PEERS, MSG, 1, LANES), SPREAD, 0, 0, tiled=True)
    return make_density(received.reshape(PEERS * MSG, LANES))


def solution(mesh):
    fine = Mesh(mesh.devices.reshape(SIZES), NAMES)
    in_specs = (P(None, WIN, None, TILE), P(), P(), P(), P())
    out_specs = (P(None, None, TILE, WIN), P(None, TILE + WIN))
    return jax.shard_map(local, mesh=fine, in_specs=in_specs, out_specs=out_specs, check_vma=False)
```

```python
import jax
import jax.numpy as jnp
import numpy as np
from jax import lax
from jax.experimental import pallas as pl
from jax.experimental.pallas import tpu as pltpu
from jax.sharding import Mesh, PartitionSpec as P

GRID_SIDE = 64
WINDOWS = 128
LANES = 128
SEGS = 32
ROWS = 16
PEERS = 64
MSG = 3 * ROWS + 1
VMEM_LIMIT = 24 * 1024 * 1024
UNROLL = 4
PAIRS = SEGS // 2
HELD = 6
NAMES = ("xl", "zh", "zl", "core", "y", "xh")
SIZES = (2, 4, 2, 2, 4, 2)
TILE = ("xl", "zh", "zl", "core")
WIN = ("y", "xh")
GATHER = ("core", "xl", "zh", "zl")
SPREAD = ("y", "xl", "xh", "zl", "core")

PEER = [(y, xl, xh, zl, core) for y in range(4) for xl in range(2) for xh in range(2) for zl in range(2) for core in range(2)]
HOLDERS = [[n for n, p in enumerate(PEER) if p[4] * 2 + p[1] == freq] for freq in range(4)]


def tile_of(run):
    return (run % 16) * 2 + run // 16


def half_turn_series():
    x = np.cos(np.linspace(0.0, np.pi, 4001)) * 0.5
    y = x * x
    powers = y[:, None] ** np.arange(5)[None, :]
    sin_c = np.linalg.lstsq(powers[:, :5], np.sqrt(2.0) * np.pi * np.sinc(x), rcond=None)[0]
    cos_c = np.linalg.lstsq(powers[:, :5], -np.sqrt(2.0) * np.cos(np.pi * x), rcond=None)[0]
    return [float(v) for v in sin_c], [float(v) for v in cos_c]


SIN_C, COS_C = half_turn_series()


def series(coefficients, y):
    total = coefficients[-1] * y + coefficients[-2]
    for c in coefficients[-3::-1]:
        total = total * y + c
    return total


def in_vmem():
    return pl.BlockSpec(memory_space=pltpu.VMEM)


def in_hbm():
    return pl.BlockSpec(memory_space=pltpu.HBM)


def keep_in_hbm(array):
    return pltpu.with_memory_space_constraint(array, pltpu.HBM)


def my_freq():
    return lax.axis_index("core") * 2 + lax.axis_index("xl")


def split(value):
    high = value.astype(jnp.bfloat16)
    low = (value - high.astype(jnp.float32)).astype(jnp.bfloat16)
    return high, low


def swap_pairs(value):
    count = value.shape[0]
    up = pltpu.roll(value, count - 1, 0)
    down = pltpu.roll(value, 1, 0)
    row = lax.broadcasted_iota(jnp.int32, value.shape, 0)
    return jnp.where(row % 2 == 0, up, -down)


def replica_kernel(pos_hbm, cand_hbm, wave_hbm, held_ref, rest_hbm, scale_ref, pos_ref, cand_ref, wave_ref, rest_ref, sem):
    pairs = ((pos_hbm, pos_ref), (cand_hbm, cand_ref), (wave_hbm, wave_ref))
    loads = [pltpu.make_async_copy(src, dst, sem.at[n]) for n, (src, dst) in enumerate(pairs)]
    for load in loads:
        load.start()
    for load in loads:
        load.wait()
    freq, zh = my_freq(), lax.axis_index("zh")
    turn = wave_ref[freq] * (0.5 / np.pi)
    cx, cz2 = [], []
    for xl in range(2):
        lanes = pl.ds(pl.multiple_of((xl * 4 + zh) * LANES, LANES), LANES)
        grids = cand_ref[:, lanes]
        bin_of = lax.broadcasted_iota(jnp.int32, grids.shape, 0)
        grid = jnp.sum(jnp.where(bin_of == freq, grids, 0), axis=0, keepdims=True)
        cx.append(((grid % GRID_SIDE).astype(jnp.float32) - GRID_SIDE / 2) * 8.0)
        depth = 50.0 + (grid // GRID_SIDE).astype(jnp.float32) * 4.0
        cz2.append(depth * depth)

    def store(pair):
        return pltpu.make_async_copy(rest_ref.at[pair], rest_hbm.at[pair], sem.at[3])

    def pair_step(pair, out_ref, out_pair, norms):
        norms = list(norms)
        for half in range(2):
            lanes = pl.ds(pl.multiple_of(tile_of(pair * 2 + half) * LANES, LANES), LANES)
            px = jnp.broadcast_to(pos_ref[0:1, lanes], (LANES, LANES)).T
            py = pos_ref[1:2, lanes]
            py2 = jnp.broadcast_to(py * py, (LANES, LANES)).T
            for xl in range(2):
                for part in range(LANES // 32):
                    own = slice(part * 32, part * 32 + 32)
                    delta = px[own] - cx[xl]
                    r2 = delta * delta + (py2[own] + cz2[xl])
                    inv = lax.rsqrt(r2)
                    turns = (r2 * inv) * turn
                    x = turns - jnp.round(turns)
                    y = x * x
                    sin = x * series(SIN_C, y)
                    most = inv * sin
                    re_h, re_l = split(inv - most * sin)
                    im_h, im_l = split(most * series(COS_C, y))
                    rows = slice(half * LANES + part * 32, half * LANES + part * 32 + 32)
                    re = slice(xl * 2 * LANES, xl * 2 * LANES + LANES)
                    im = slice(xl * 2 * LANES + LANES, xl * 2 * LANES + 2 * LANES)
                    out_ref[out_pair, 0, rows, re] = re_h
                    out_ref[out_pair, 1, rows, re] = re_l
                    out_ref[out_pair, 0, rows, im] = im_h
                    out_ref[out_pair, 1, rows, im] = im_l
                    amp2 = inv * inv
                    norms[xl] += (amp2[0:8] + amp2[8:16]) + (amp2[16:24] + amp2[24:32])
        return tuple(norms)

    def rest_step(pair, norms):
        norms = pair_step(pair + HELD, rest_ref, pair, norms)
        store(pair).start()
        return norms

    norms = (jnp.zeros((8, LANES), jnp.float32),) * 2
    norms = lax.fori_loop(0, PAIRS - HELD, rest_step, norms, unroll=UNROLL)
    norms = lax.fori_loop(0, HELD, lambda pair, norms: pair_step(pair, held_ref, pair, norms), norms, unroll=UNROLL)
    for xl in range(2):
        norm = jnp.sum(norms[xl], axis=0, keepdims=True)
        scale_ref[xl] = jnp.broadcast_to(1.0 / (WINDOWS * norm), (8, LANES))

    @pl.loop(0, PAIRS - HELD)
    def _(pair):
        store(pair).wait()


def make_replicas(positions, cands, wavenumbers):
    held = jax.ShapeDtypeStruct((HELD, 2, 2 * LANES, 4 * LANES), jnp.bfloat16)
    rest = pltpu.HBM((PAIRS - HELD, 2, 2 * LANES, 4 * LANES), jnp.bfloat16)
    return pl.pallas_call(
        replica_kernel,
        out_shape=(held, rest, jax.ShapeDtypeStruct((2, 8, LANES), jnp.float32)),
        in_specs=[in_hbm()] * 3,
        out_specs=(in_vmem(), in_hbm(), in_vmem()),
        scratch_shapes=[
            pltpu.VMEM(positions.shape, jnp.float32),
            pltpu.VMEM(cands.shape, jnp.int32),
            pltpu.SMEM(wavenumbers.shape, jnp.float32),
            pltpu.VMEM(rest.shape, jnp.bfloat16),
            pltpu.SemaphoreType.DMA((4,)),
        ],
        compiler_params=pltpu.CompilerParams(vmem_limit_bytes=VMEM_LIMIT),
        cost_estimate=pl.CostEstimate(flops=60_000_000, bytes_accessed=10_000_000, transcendentals=1_000_000),
        name="replicas",
    )(*[keep_in_hbm(array) for array in (positions, cands, wavenumbers)])


def message_kernel(order_ref, spec_ref, held_ref, rest_hbm, scale_ref, out_ref, ordered, rest_ref, sem):
    zh = lax.axis_index("zh")
    loads = [pltpu.make_async_copy(rest_hbm.at[n], rest_ref.at[n], sem.at[n]) for n in range(PAIRS - HELD)]
    for load in loads:
        load.start()
    proj = jnp.zeros((ROWS, 4 * LANES), jnp.float32)
    for some in range(SEGS // 4):
        for seg in range(some * 4, some * 4 + 4):
            index = jnp.broadcast_to(order_ref[seg:seg + 1, :], (8, LANES))
            lane = index % LANES
            home = index // LANES
            total = [jnp.zeros((8, LANES), jnp.float32) for _ in range(ROWS // 8)]
            for run in range(SEGS):
                here = home == tile_of(run)
                for part in range(ROWS // 8):
                    there = jnp.take_along_axis(spec_ref[run, part * 8:part * 8 + 8, :], lane, axis=1)
                    total[part] = jnp.where(here, there, total[part])
            for part in range(ROWS // 8):
                ordered[seg, part * 8:part * 8 + 8, :] = total[part]
        for pair in range(some * 2, some * 2 + 2):
            data = jnp.concatenate([spec_ref[pair * 2], spec_ref[pair * 2 + 1]], axis=1)
            data_h, data_l = split(data)
            both = jnp.concatenate([data_h, data_l], axis=0)
            if pair < HELD:
                high, low = held_ref[pair, 0], held_ref[pair, 1]
            else:
                loads[pair - HELD].wait()
                high, low = rest_ref[pair - HELD, 0], rest_ref[pair - HELD, 1]
            first = jnp.dot(both, high, preferred_element_type=jnp.float32)
            second = jnp.dot(data_h, low, preferred_element_type=jnp.float32)
            proj += first[:ROWS] + first[ROWS:] + second

    powers = []
    for xl in range(2):
        real = proj[:, xl * 2 * LANES:xl * 2 * LANES + LANES]
        value = real + swap_pairs(proj[:, xl * 2 * LANES + LANES:xl * 2 * LANES + 2 * LANES])
        powers.append(jnp.sum(value * value, axis=0, keepdims=True) * scale_ref[xl, 0:1, :])
    for peer, (y, xl, xh, zl, core) in enumerate(PEER):
        start = peer * MSG
        out_ref[start:start + ROWS, :] = ordered[xl * 16 + zh * 4 + zl * 2 + core]
        for run in range(2):
            place = slice(start + (1 + run) * ROWS, start + (2 + run) * ROWS)
            out_ref[place, :] = ordered[(y * 2 + xh) * 4 + core * 2 + run]
        out_ref[start + 3 * ROWS:start + MSG, :] = jnp.broadcast_to(powers[xl], (MSG - 3 * ROWS, LANES))


def make_messages(order, spec, held, rest, scale):
    return pl.pallas_call(
        message_kernel,
        out_shape=jax.ShapeDtypeStruct((PEERS * MSG, LANES), jnp.float32),
        in_specs=[in_vmem(), in_vmem(), in_vmem(), in_hbm(), in_vmem()],
        out_specs=in_vmem(),
        scratch_shapes=[
            pltpu.VMEM((SEGS, ROWS, LANES), jnp.float32),
            pltpu.VMEM(rest.shape, rest.dtype),
            pltpu.SemaphoreType.DMA((PAIRS - HELD,)),
        ],
        compiler_params=pltpu.CompilerParams(vmem_limit_bytes=VMEM_LIMIT),
        cost_estimate=pl.CostEstimate(flops=100_000_000, bytes_accessed=10_000_000, transcendentals=0),
        name="messages",
    )(order, spec, held, keep_in_hbm(rest), scale)


def gather_rows(ref, freq, start):
    each = ref.shape[0] // PEERS
    return jnp.concatenate([ref[n * each + start:n * each + start + ROWS, :] for n in HOLDERS[freq]], axis=0)


def product(left_h, left_l, ref, freq, start):
    parts = [gather_rows(ref, freq, start + run * ROWS) for run in range(2)]
    right_h, right_l = split(jnp.concatenate(parts, axis=1))
    total = jnp.dot(left_h, right_h, preferred_element_type=jnp.float32)
    total += jnp.dot(left_h, right_l, preferred_element_type=jnp.float32)
    return total + jnp.dot(left_l, right_h, preferred_element_type=jnp.float32)


def send_out(freq, half, total, stage, out_ref, sem):
    columns = pl.ds(pl.multiple_of(half * 2 * LANES, 2 * LANES), 2 * LANES)
    copies = []
    for piece in range(4):
        part, rows = piece // 2, pl.ds(piece % 2 * 64, 64)
        stage[freq, part, rows, :] = total[piece * 64:(piece + 1) * 64]
        source, target = stage.at[freq, part, rows], out_ref.at[freq, part, rows, columns]
        copy = pltpu.make_async_copy(source, target, sem.at[freq * 4 + piece])
        copy.start()
        copies.append(copy)
    return copies


def column_kernel(got_ref, out_ref):
    for n in range(PEERS):
        out_ref[n * 2 * ROWS:(n + 1) * 2 * ROWS, :] = got_ref[n * MSG + ROWS:n * MSG + 3 * ROWS, :]


def take_columns(received):
    return pl.pallas_call(
        column_kernel,
        out_shape=jax.ShapeDtypeStruct((PEERS * 2 * ROWS, LANES), jnp.float32),
        in_specs=[in_vmem()],
        out_specs=in_vmem(),
        compiler_params=pltpu.CompilerParams(vmem_limit_bytes=VMEM_LIMIT),
        name="columns",
    )(received)


def own_density_kernel(got_ref, out_ref, high_ref, low_ref, beam_ref, stage, sem):
    mine = (lax.axis_index(("zl", "core")) * 8 + lax.axis_index(WIN)) * 4
    for freq in range(4):
        shares = [got_ref[n * MSG + 3 * ROWS:n * MSG + 3 * ROWS + 1, :] for n in HOLDERS[freq]]
        while len(shares) > 1:
            shares = [a + b for a, b in zip(shares[::2], shares[1::2])]
        beam_ref[freq:freq + 1, :] = pltpu.roll(shares[0], lax.rem(LANES - mine, LANES), 1)[:, 0:4]
    copies = []
    for freq in range(4):
        rows = gather_rows(got_ref, freq, 0) * (1.0 / WINDOWS)
        left = jnp.concatenate([rows, swap_pairs(rows)], axis=1)
        left_h, left_l = split(left.T)
        high_ref[freq] = left_h
        low_ref[freq] = left_l
        total = product(left_h, left_l, got_ref, freq, ROWS)
        copies.extend(send_out(freq, lax.axis_index("core"), total, stage, out_ref, sem))
    for copy in copies:
        copy.wait()


def other_density_kernel(high_ref, low_ref, got_ref, base_ref, out_ref, stage, sem):
    del base_ref
    copies = []
    for freq in range(4):
        total = product(high_ref[freq], low_ref[freq], got_ref, freq, 0)
        copies.extend(send_out(freq, 1 - lax.axis_index("core"), total, stage, out_ref, sem))
    for copy in copies:
        copy.wait()


def make_density(received):
    density = jax.ShapeDtypeStruct((4, 2, LANES, 4 * LANES), jnp.float32)
    left = jax.ShapeDtypeStruct((4, 2 * LANES, 2 * LANES), jnp.bfloat16)
    scratch = [pltpu.VMEM((4, 2, LANES, 2 * LANES), jnp.float32), pltpu.SemaphoreType.DMA((16,))]
    params = pltpu.CompilerParams(vmem_limit_bytes=VMEM_LIMIT)
    cost = pl.CostEstimate(flops=800_000_000, bytes_accessed=5_000_000, transcendentals=0)
    anywhere = in_hbm()
    half, high, low, beam = pl.pallas_call(
        own_density_kernel,
        out_shape=(density, left, left, jax.ShapeDtypeStruct((4, 4), jnp.float32)),
        in_specs=[in_vmem()],
        out_specs=(anywhere, in_vmem(), in_vmem(), in_vmem()),
        scratch_shapes=scratch,
        compiler_params=params,
        cost_estimate=cost,
        name="own_density",
    )(received)
    other = lax.ppermute(take_columns(received), "core", [(0, 1), (1, 0)])
    density = pl.pallas_call(
        other_density_kernel,
        out_shape=density,
        in_specs=[in_vmem(), in_vmem(), in_vmem(), anywhere],
        out_specs=anywhere,
        scratch_shapes=scratch,
        input_output_aliases={3: 0},
        compiler_params=params,
        cost_estimate=cost,
        name="other_density",
    )(high, low, other, half)
    return density, beam


def local(spectra, sensor_positions, wavenumbers, sensor_order, candidates):
    parts = spectra.reshape(2, 2, 1, 2, ROWS, LANES)
    outgoing = jnp.broadcast_to(parts, (2, 2, 4, 2, ROWS, LANES))
    gathered = lax.all_to_all(outgoing.reshape(SEGS, ROWS, LANES), GATHER, 0, 0, tiled=True)
    held, rest, scale = make_replicas(sensor_positions, candidates, wavenumbers)
    messages = make_messages(sensor_order.reshape(SEGS, LANES), gathered, held, rest, scale)
    received = lax.all_to_all(messages.reshape(PEERS, MSG, 1, LANES), SPREAD, 0, 0, tiled=True)
    return make_density(received.reshape(PEERS * MSG, LANES))


def solution(mesh):
    fine = Mesh(mesh.devices.reshape(SIZES), NAMES)
    in_specs = (P(None, WIN, None, TILE), P(), P(), P(), P())
    out_specs = (P(None, None, TILE, WIN), P(None, TILE + WIN))
    return jax.shard_map(local, mesh=fine, in_specs=in_specs, out_specs=out_specs, check_vma=False)
```
